1024 devices in a mesh: tower: 2 (over core), dp: 32 (over x, z_lo), tensor: 16 (over z_hi, y).
Axes of the slice: x: 4, y: 4, z: 32 (z_hi: 4, z_lo: 8; z = z_hi * 8 + z_lo), core: 2. Of those that a mesh axis runs over, the one named last changes fastest.
Arguments:
- text_query: bfloat16 [2, 8, 64, 64, 128], P('tower', None, 'tensor'), may hold values from -6 to 6
- attn_out: bfloat16 [2, 8, 64, 64, 128], P('tower', None, 'tensor'), may hold values from -6 to 6
- grad_out: bfloat16 [2, 8, 64, 64, 128], P('tower', None, 'tensor'), may hold values from -6 to 6
- log_norm: bfloat16 [2, 8, 64, 64], P('tower', None, 'tensor'), may hold values from 2.5 to 4.5
- image_keys: bfloat16 [2, 26624, 1024], P('tower', ('dp', 'tensor')), may hold values from -6 to 6
- image_values: bfloat16 [2, 26624, 1024], P('tower', ('dp', 'tensor')), may hold values from -6 to 6
- k_weight: bfloat16 [2, 8192, 1024], P('tower', 'tensor'), may hold values from -0.0625 to 0.0625
- v_weight: bfloat16 [2, 8192, 1024], P('tower', 'tensor'), may hold values from -0.0625 to 0.0625
- layer_gate: float32 [2], P('tower'), may hold values from 0.3 to 1.2
- tile_counts: int32 [8], replicated, may hold values from 1 to 2, as said below
- text_lens: int32 [8], replicated, may hold values from 1 to 64, as said below
Outputs:
- feat_grad: float32 [26624, 8192], P(('dp', 'tensor'), 'tower')
The draws below stay inside these ranges and needn't reach their ends.
Inputs may be any that keep to these rules, and one draw needn't show every extreme that they name: `tile_counts`: some sample has 2 tiles. `text_lens`: some sample has 64 text tokens.
All inputs are finite; a program needn't handle non-finite values.
Results may differ from the reference program's by a relative error of at most 0.025.
Values may be sent and summed in bfloat16 or wider, within the bound.
No kernel may reach another device: no remote copies, remote signals or barrier semaphores. Data moves between devices by JAX's collectives and lax.ppermute only.
A program may use at most 64 MiB of HBM per device.

```python
import math
import jax
import jax.numpy as jnp
from jax import lax

H = 64
KVH = 8
HD = 128
VD = 8192
TXT = 64
TILES = 2
TILE_LEN = 1601
TILE_PAD = 1664
LAYERS = 2
BATCH = 8
S_IMG = 3328
S_ALL = 26624
KVW = 1024


def draw_tile_counts(key, part):
    key = jax.random.fold_in(key, 11)
    key_values, key_where = jax.random.split(key)
    drawn = jax.random.randint(key_values, (BATCH,), 1, TILES + 1)
    chosen = jax.random.randint(key_where, (), 0, BATCH)
    return jnp.where(jnp.arange(BATCH) == chosen, TILES, drawn).astype(jnp.int32)


def draw_text_lens(key, part):
    key = jax.random.fold_in(key, 23)
    key_values, key_where = jax.random.split(key)
    drawn = jax.random.randint(key_values, (BATCH,), 1, TXT + 1)
    chosen = jax.random.randint(key_where, (), 0, BATCH)
    return jnp.where(jnp.arange(BATCH) == chosen, TXT, drawn).astype(jnp.int32)


def steps_of(stream_key, dims, pieces, least, top_value):
    level, own = 1.0, jax.random.fold_in(stream_key, 6)
    for dim, parts in pieces:
        draws = jnp.exp(jax.random.uniform(jax.random.fold_in(own, dim), (parts,), jnp.float32, least / len(pieces), top_value / len(pieces)))
        level = level * jnp.repeat(draws, dims[dim] // parts).reshape([-1 if axis == dim else 1 for axis in range(len(dims))])
    return level


def scatter_about(own_key, dims, scale, limit, cuts=(), dtype=jnp.bfloat16):
    values = scale * jax.random.normal(own_key, dims, jnp.float32)
    if cuts:
        values = values * steps_of(own_key, dims, cuts, -0.22, 0.18)
    return jnp.clip(values, -limit, limit).astype(dtype)


def setup_inputs(seed: int = 0) -> dict:
    splits = jax.random.split(jax.random.key(seed), 12)
    return {
        "text_query": scatter_about(splits[0], (LAYERS, BATCH, H, TXT, HD), 1.0, 6.0, ((0, 2), (2, 16))),
        "attn_out": scatter_about(splits[1], (LAYERS, BATCH, H, TXT, HD), 1.0, 6.0, ((0, 2), (2, 16))),
        "grad_out": scatter_about(splits[2], (LAYERS, BATCH, H, TXT, HD), 1.0, 6.0, ((0, 2), (2, 16))),
        "log_norm": jnp.clip(2.5 + 2.0 * jax.random.uniform(splits[3], (LAYERS, BATCH, H, TXT), jnp.float32) ** steps_of(splits[3], (LAYERS, BATCH, H, TXT), ((0, 2), (2, 16)), -0.2, 0.2), 2.5, 4.5).astype(jnp.bfloat16),
        "image_keys": scatter_about(splits[4], (LAYERS, S_ALL, KVW), 1.0, 6.0, ((0, 2), (1, 512))),
        "image_values": scatter_about(splits[5], (LAYERS, S_ALL, KVW), 1.0, 6.0, ((0, 2), (1, 512))),
        "k_weight": scatter_about(splits[6], (LAYERS, VD, KVW), VD ** -0.5, 0.0625, ((0, 2), (1, 16))),
        "v_weight": scatter_about(splits[7], (LAYERS, VD, KVW), VD ** -0.5, 0.0625, ((0, 2), (1, 16))),
        "layer_gate": jnp.clip(0.3 + 0.90000004 * jax.random.uniform(splits[8], (LAYERS,), jnp.float32) ** steps_of(splits[8], (LAYERS,), ((0, 2),), -0.2, 0.2), 0.3, 1.2),
        "tile_counts": draw_tile_counts(jax.random.fold_in(splits[11], 71), 0),
        "text_lens": draw_text_lens(jax.random.fold_in(splits[11], 71), 0),
    }


def sample_grads(text_query, attn_out, grad_out, log_norm, image_keys, image_values, tiles, length, gain):
    row_mask = (jnp.arange(TXT) < length).astype(jnp.float32)
    scaled_grad = (gain * grad_out.astype(jnp.float32) * row_mask[None, :, None]).astype(jnp.bfloat16)
    scaled_wide = lax.optimization_barrier(scaled_grad).astype(jnp.float32)
    row_delta = lax.optimization_barrier(jnp.sum(scaled_wide * attn_out.astype(jnp.float32), axis=-1)).astype(jnp.bfloat16)
    delta_wide = lax.optimization_barrier(row_delta).astype(jnp.float32)
    position = jnp.arange(S_IMG)
    key_mask = ((position // TILE_PAD < tiles) & (position % TILE_PAD < TILE_LEN)).astype(jnp.float32)
    group_size = H // KVH
    scaling = 1.0 / math.sqrt(HD)
    queries = text_query.astype(jnp.float32).reshape(KVH, group_size, TXT, HD)
    grads = scaled_wide.reshape(KVH, group_size, TXT, HD)
    keys_split = image_keys.astype(jnp.float32).reshape(S_IMG, KVH, HD)
    values_split = image_values.astype(jnp.float32).reshape(S_IMG, KVH, HD)
    norms = log_norm.astype(jnp.float32).reshape(KVH, group_size, TXT)
    deltas = delta_wide.reshape(KVH, group_size, TXT)
    highest = lax.Precision.HIGHEST
    scores = jnp.einsum('kgrd,pkd->kgrp', queries, keys_split, precision=highest) * scaling
    attention = jnp.exp(scores - norms[..., None]) * key_mask
    attention_b = lax.optimization_barrier(attention.astype(jnp.bfloat16)).astype(jnp.float32)
    value_grad = jnp.einsum('kgrp,kgrd->pkd', attention_b, grads, precision=highest)
    grad_probs = jnp.einsum('kgrd,pkd->kgrp', grads, values_split, precision=highest)
    grad_scores = (attention * (grad_probs - deltas[..., None])).astype(jnp.bfloat16)
    grad_wide = lax.optimization_barrier(grad_scores).astype(jnp.float32)
    key_grad = jnp.einsum('kgrp,kgrd->pkd', grad_wide, queries, precision=highest) * scaling
    return (key_grad.reshape(S_IMG, KVW).astype(jnp.bfloat16), value_grad.reshape(S_IMG, KVW).astype(jnp.bfloat16))

def reference(text_query, attn_out, grad_out, log_norm, image_keys, image_values, k_weight, v_weight, layer_gate, tile_counts, text_lens):
    feat_grad = jnp.zeros((BATCH, S_IMG, VD), jnp.float32)
    keys_all = image_keys.reshape(LAYERS, BATCH, S_IMG, KVW)
    values_all = image_values.reshape(LAYERS, BATCH, S_IMG, KVW)
    for layer_id in range(LAYERS):
        gain = jnp.tanh(layer_gate[layer_id])
        k_mat = k_weight[layer_id]
        v_mat = v_weight[layer_id]

        def one_sample(inputs):
            tq, ao, go, ln, ik, iv, tiles, length = inputs
            key_grad, value_grad = sample_grads(tq, ao, go, ln, ik, iv, tiles, length, gain)
            return jnp.dot(key_grad, k_mat.T, preferred_element_type=jnp.float32) + jnp.dot(value_grad, v_mat.T, preferred_element_type=jnp.float32)
        layer_feat = lax.map(one_sample, (text_query[layer_id], attn_out[layer_id], grad_out[layer_id], log_norm[layer_id], keys_all[layer_id], values_all[layer_id], tile_counts, text_lens))
        feat_grad = feat_grad + layer_feat
    return feat_grad.reshape(BATCH * S_IMG, VD)
```

```python
import math

import jax
import jax.numpy as jnp
from jax import lax
from jax.experimental import pallas as pl
from jax.experimental.pallas import tpu as pltpu
from jax.sharding import Mesh, PartitionSpec as P

H = 64
KVH = 8
HD = 128
TXT = 64
TILE_LEN = 1601
TILE_PAD = 1664
NAMES = ("core", "x", "zb", "zq", "zh", "y")
SIZES = (2, 4, 2, 4, 4, 4)
SCALING = 1.0 / math.sqrt(HD)
LOCAL = H // 16
QROWS = LOCAL * TXT
META = 2 * QROWS
PACK = META + 16
NT = (((1,), (1,)), ((), ()))
NN = (((1,), (0,)), ((), ()))


def attention_kernel(pack_ref, key_ref, value_ref, mask_ref, out_ref):
    query = pack_ref[:, 0, 0:QROWS, :].reshape(2 * QROWS, HD)
    grad = pack_ref[:, 0, QROWS : 2 * QROWS, :].reshape(2 * QROWS, HD)
    meta = pack_ref[:, 0, META : META + 16, :].astype(jnp.float32)
    norm = jnp.concatenate([meta[i, j : j + 1] for i in range(2) for j in (0, 1)], axis=1)
    delta = jnp.concatenate([meta[i, j : j + 1] for i in range(2) for j in (2, 3)], axis=1)
    mask = mask_ref[...]
    scores = lax.dot_general(key_ref[0], query, NT, preferred_element_type=jnp.float32) * SCALING
    attention = jnp.exp(scores - norm) * mask
    out_ref[1] = lax.dot_general(
        attention.astype(jnp.bfloat16), grad, NN, preferred_element_type=jnp.float32
    ).astype(jnp.bfloat16)
    probs = lax.dot_general(value_ref[0], grad, NT, preferred_element_type=jnp.float32)
    grad_scores = (attention * (probs - delta)).astype(jnp.bfloat16)
    out_ref[0] = (
        lax.dot_general(grad_scores, query, NN, preferred_element_type=jnp.float32) * SCALING
    ).astype(jnp.bfloat16)


def attention_grads(packed, keys, values, mask):
    rows = keys.shape[1]
    block = pl.BlockSpec((1, rows, HD), lambda g: (0, 0, g))
    return pl.pallas_call(
        attention_kernel,
        grid=(KVH,),
        in_specs=[
            pl.BlockSpec((2, 1, PACK, HD), lambda g: (g % 2, g // 2, 0, 0)),
            block,
            block,
            pl.BlockSpec((rows, 1), lambda g: (0, 0)),
        ],
        out_specs=pl.BlockSpec((2, rows, HD), lambda g: (0, 0, g)),
        out_shape=jax.ShapeDtypeStruct((2, rows, KVH * HD), jnp.bfloat16),
        compiler_params=pltpu.CompilerParams(vmem_limit_bytes=16 * 1024 * 1024),
        cost_estimate=pl.CostEstimate(
            flops=8 * rows * H * TXT * HD, bytes_accessed=3 << 20, transcendentals=rows * H * TXT
        ),
    )(packed, keys, values, mask)


def body(
    text_query,
    attn_out,
    grad_out,
    log_norm,
    image_keys,
    image_values,
    k_weight,
    v_weight,
    layer_gate,
    tile_counts,
    text_lens,
):
    x = lax.axis_index("x")
    zb = lax.axis_index("zb")
    zq = lax.axis_index("zq")
    zh = lax.axis_index("zh")
    y = lax.axis_index("y")
    sample = x * 2 + zb

    feature = x * 128 + (zb * 4 + zq) * 16
    weight = jnp.concatenate(
        [
            lax.dynamic_slice_in_dim(k_weight[0], feature, 16, 0),
            lax.dynamic_slice_in_dim(v_weight[0], feature, 16, 0),
        ],
        axis=1,
    )
    weight = lax.all_gather(weight, ("zh", "zb", "zq"), axis=0, tiled=True)

    query = lax.dynamic_index_in_dim(text_query[0], sample, 0, keepdims=False)
    out = lax.dynamic_index_in_dim(attn_out[0], sample, 0, keepdims=False)
    cot = lax.dynamic_index_in_dim(grad_out[0], sample, 0, keepdims=False)
    norm = lax.dynamic_index_in_dim(log_norm[0], sample, 0, keepdims=False)
    row_mask = (jnp.arange(TXT) < text_lens[sample]).astype(jnp.float32)
    scaled = (jnp.tanh(layer_gate[0]) * cot.astype(jnp.float32) * row_mask[None, :, None]).astype(
        jnp.bfloat16
    )
    delta = jnp.sum(scaled.astype(jnp.float32) * out.astype(jnp.float32), axis=-1).astype(
        jnp.bfloat16
    )
    packed = jnp.concatenate(
        [
            query.reshape(QROWS, HD),
            scaled.reshape(QROWS, HD),
            norm.reshape(QROWS // HD, HD),
            delta.reshape(QROWS // HD, HD),
            jnp.zeros((16 - 2 * (QROWS // HD), HD), jnp.bfloat16),
        ],
        axis=0,
    )
    packed = lax.all_gather(packed, "zh", axis=0, tiled=False)
    packed = jnp.broadcast_to(packed[None], (4, 4, PACK, HD))
    packed = lax.all_to_all(packed, "y", split_axis=0, concat_axis=0, tiled=True)

    rows = image_keys.shape[1]
    position = (zq * 16 + zh * 4 + y) * rows + jnp.arange(rows)
    key_mask = (
        (position // TILE_PAD < tile_counts[sample]) & (position % TILE_PAD < TILE_LEN)
    ).astype(jnp.float32)
    grads = attention_grads(packed, image_keys, image_values, key_mask[:, None])

    both = jnp.concatenate([grads[0], grads[1]], axis=1)
    both = jnp.broadcast_to(both[None], (16, rows, 2 * KVH * HD))
    both = lax.all_to_all(both, ("x", "y"), split_axis=0, concat_axis=0, tiled=True)
    both = both.reshape(16 * rows, 2 * KVH * HD)
    halves = weight.reshape(2, 256, 2 * KVH * HD)
    part = jnp.stack(
        [
            lax.dot_general(both, halves[t], NT, preferred_element_type=jnp.float32).astype(
                jnp.bfloat16
            )
            for t in range(2)
        ]
    )
    part = part.reshape(32, rows, 256)
    part = lax.all_to_all(part, ("core", "x", "y"), split_axis=0, concat_axis=0, tiled=True)
    part = part.reshape(2, 4, 4, rows, 2, HD).astype(jnp.float32)
    total = part[0] + part[1]
    return total.transpose(2, 3, 1, 0, 4).reshape(rows, 2 * 4 * 4 * HD)


def solution(mesh):
    fine = Mesh(mesh.devices.reshape(SIZES), NAMES)
    tensor = ("zh", "y")
    rows = ("x", "zb", "zq", "zh", "y")
    in_specs = (
        P("core", None, tensor, None, None),
        P("core", None, tensor, None, None),
        P("core", None, tensor, None, None),
        P("core", None, tensor, None),
        P("core", rows, None),
        P("core", rows, None),
        P("core", tensor, None),
        P("core", tensor, None),
        P("core"),
        P(),
        P(),
    )
    return jax.shard_map(
        body, mesh=fine, in_specs=in_specs, out_specs=P(rows, "core"), check_vma=False
    )
```

```python
import math

import jax
import jax.numpy as jnp
from jax import lax
from jax.experimental import pallas as pl
from jax.experimental.pallas import tpu as pltpu
from jax.sharding import Mesh, PartitionSpec as P

H = 64
KVH = 8
HD = 128
TXT = 64
TILE_LEN = 1601
TILE_PAD = 1664
NAMES = ("core", "x", "zb", "zq", "zh", "y")
SIZES = (2, 4, 2, 4, 4, 4)
SCALING = 1.0 / math.sqrt(HD)
LOCAL = H // 16
QROWS = LOCAL * TXT
META = 2 * QROWS
PACK = META + 16
NT = (((1,), (1,)), ((), ()))
NN = (((1,), (0,)), ((), ()))


def attention_kernel(block_ref, pack_ref, key_ref, value_ref, mask_ref, done_ref, out_ref):
    del block_ref, done_ref
    query = pack_ref[:, 0:QROWS, :].reshape(2 * QROWS, HD)
    grad = pack_ref[:, QROWS : 2 * QROWS, :].reshape(2 * QROWS, HD)
    meta = pack_ref[:, META : META + 16, :].astype(jnp.float32)
    norm = jnp.concatenate([meta[i, j : j + 1] for i in range(2) for j in (0, 1)], axis=1)
    delta = jnp.concatenate([meta[i, j : j + 1] for i in range(2) for j in (2, 3)], axis=1)
    mask = mask_ref[...]
    scores = lax.dot_general(key_ref[...], query, NT, preferred_element_type=jnp.float32) * SCALING
    attention = jnp.exp(scores - norm) * mask
    out_ref[1] = lax.dot_general(
        attention.astype(jnp.bfloat16), grad, NN, preferred_element_type=jnp.float32
    ).astype(jnp.bfloat16)
    probs = lax.dot_general(value_ref[...], grad, NT, preferred_element_type=jnp.float32)
    grad_scores = (attention * (probs - delta)).astype(jnp.bfloat16)
    out_ref[0] = (
        lax.dot_general(grad_scores, query, NN, preferred_element_type=jnp.float32) * SCALING
    ).astype(jnp.bfloat16)


def attention_grads(block, packed, keys, values, mask, done):
    rows = keys.shape[0]
    head = pl.BlockSpec((rows, HD), lambda p, b: (0, 2 * b[0] + p))
    return pl.pallas_call(
        attention_kernel,
        grid_spec=pltpu.PrefetchScalarGridSpec(
            num_scalar_prefetch=1,
            grid=(2,),
            in_specs=[
                pl.BlockSpec((2, PACK, HD), lambda p, b: (p, 0, 0)),
                head,
                head,
                pl.BlockSpec((rows, 1), lambda p, b: (0, 0)),
                pl.BlockSpec(memory_space=pl.ANY),
            ],
            out_specs=pl.BlockSpec((2, rows, HD), lambda p, b: (0, 0, 2 * b[0] + p)),
        ),
        out_shape=jax.ShapeDtypeStruct((2, rows, KVH * HD), jnp.bfloat16),
        input_output_aliases={5: 0},
        compiler_params=pltpu.CompilerParams(vmem_limit_bytes=16 * 1024 * 1024),
        cost_estimate=pl.CostEstimate(
            flops=2 * rows * H * TXT * HD, bytes_accessed=1 << 20, transcendentals=rows * H * TXT // 4
        ),
    )(block, packed, keys, values, mask, done)


def body(
    text_query,
    attn_out,
    grad_out,
    log_norm,
    image_keys,
    image_values,
    k_weight,
    v_weight,
    layer_gate,
    tile_counts,
    text_lens,
):
    x = lax.axis_index("x")
    zb = lax.axis_index("zb")
    zq = lax.axis_index("zq")
    zh = lax.axis_index("zh")
    y = lax.axis_index("y")
    sample = x * 2 + zb

    feature = x * 128 + (zb * 4 + zq) * 16
    weight = jnp.concatenate(
        [
            lax.dynamic_slice_in_dim(k_weight[0], feature, 16, 0),
            lax.dynamic_slice_in_dim(v_weight[0], feature, 16, 0),
        ],
        axis=1,
    )
    weight = lax.all_gather(weight, ("zh", "zb", "zq"), axis=0, tiled=True)

    query = lax.dynamic_index_in_dim(text_query[0], sample, 0, keepdims=False)
    out = lax.dynamic_index_in_dim(attn_out[0], sample, 0, keepdims=False)
    cot = lax.dynamic_index_in_dim(grad_out[0], sample, 0, keepdims=False)
    norm = lax.dynamic_index_in_dim(log_norm[0], sample, 0, keepdims=False)
    row_mask = (jnp.arange(TXT) < text_lens[sample]).astype(jnp.float32)
    scaled = (jnp.tanh(layer_gate[0]) * cot.astype(jnp.float32) * row_mask[None, :, None]).astype(
        jnp.bfloat16
    )
    delta = jnp.sum(scaled.astype(jnp.float32) * out.astype(jnp.float32), axis=-1).astype(
        jnp.bfloat16
    )
    packed = jnp.concatenate(
        [
            query.reshape(QROWS, HD),
            scaled.reshape(QROWS, HD),
            norm.reshape(QROWS // HD, HD),
            delta.reshape(QROWS // HD, HD),
            jnp.zeros((16 - 2 * (QROWS // HD), HD), jnp.bfloat16),
        ],
        axis=0,
    )
    rows = image_keys.shape[1]
    padded = -(-rows // 8) * 8
    row = jnp.arange(padded)
    position = (zq * 16 + zh * 4 + y) * rows + row
    key_mask = (
        (position // TILE_PAD < tile_counts[sample])
        & (position % TILE_PAD < TILE_LEN)
        & (row < rows)
    ).astype(jnp.float32)
    keys = jnp.pad(image_keys[0], ((0, padded - rows), (0, 0)))
    values = jnp.pad(image_values[0], ((0, padded - rows), (0, 0)))
    nothing = jnp.zeros((2, padded, KVH * HD), jnp.bfloat16)

    def attend(packed):
        grads = nothing
        for shift in (0, 1, 3, 2):
            piece = packed
            if shift:
                piece = lax.ppermute(packed, "zh", [(i, (i + shift) % 4) for i in range(4)])
            piece = jnp.broadcast_to(piece[None], (4, PACK, HD))
            piece = lax.all_to_all(piece, "y", split_axis=0, concat_axis=0, tiled=True)
            block = ((zh - shift) % 4).astype(jnp.int32).reshape(1)
            grads = attention_grads(block, piece, keys, values, key_mask[:, None], grads)
        return grads

    grads = lax.cond(jnp.max(text_lens) > 0, attend, lambda _: nothing, packed)

    both = jnp.concatenate([grads[0], grads[1]], axis=1)
    both = jnp.broadcast_to(both[None], (16, padded, 2 * KVH * HD))
    both = lax.all_to_all(both, ("x", "y"), split_axis=0, concat_axis=0, tiled=True)
    both = both.reshape(16 * padded, 2 * KVH * HD)
    halves = weight.reshape(2, 256, 2 * KVH * HD)
    part = jnp.stack(
        [
            lax.dot_general(both, halves[t], NT, preferred_element_type=jnp.float32).astype(
                jnp.bfloat16
            )
            for t in range(2)
        ]
    )
    part = part.reshape(32, padded, 256)
    part = lax.all_to_all(part, ("core", "x", "y"), split_axis=0, concat_axis=0, tiled=True)
    part = part.reshape(2, 4, 4, padded, 2, HD).astype(jnp.float32)
    total = (part[0] + part[1])[:, :, :rows]
    return total.transpose(2, 3, 1, 0, 4).reshape(rows, 2 * 4 * 4 * HD)


def solution(mesh):
    fine = Mesh(mesh.devices.reshape(SIZES), NAMES)
    tensor = ("zh", "y")
    rows = ("x", "zb", "zq", "zh", "y")
    in_specs = (
        P("core", None, tensor, None, None),
        P("core", None, tensor, None, None),
        P("core", None, tensor, None, None),
        P("core", None, tensor, None),
        P("core", rows, None),
        P("core", rows, None),
        P("core", tensor, None),
        P("core", tensor, None),
        P("core"),
        P(),
        P(),
    )
    return jax.shard_map(
        body, mesh=fine, in_specs=in_specs, out_specs=P(rows, "core"), check_vma=False
    )
```

```python
import math

import jax
import jax.numpy as jnp
from jax import lax
from jax.experimental import pallas as pl
from jax.experimental.pallas import tpu as pltpu
from jax.sharding import Mesh, PartitionSpec as P

KVH = 8
HD = 128
TXT = 64
TILE_LEN = 1601
TILE_PAD = 1664
NAMES = ("core", "x", "zb", "zq", "zh", "y")
SIZES = (2, 4, 2, 4, 4, 4)
SCALING = 1.0 / math.sqrt(HD)
META = 2 * TXT
PACK = META + 16
ROWS = 52
GROUP = 8 * TXT
SLICE = 16
NT = (((1,), (1,)), ((), ()))
NN = (((1,), (0,)), ((), ()))
VMEM_LIMIT = 16 * 1024 * 1024


def prepare_kernel(
    gate_ref,
    length_ref,
    query_ref,
    out_ref,
    cot_ref,
    norm_ref,
    key_weight_ref,
    value_weight_ref,
    pack_ref,
    weight_ref,
    query,
    out,
    cot,
    key_weight,
    value_weight,
    sems,
):
    x, zb, zq = (lax.axis_index(name) for name in ("x", "zb", "zq"))
    sample = x * 2 + zb
    feature = pl.multiple_of(x * 128 + (zb * 4 + zq) * SLICE, SLICE)
    copies = [
        pltpu.make_async_copy(source, target, sems.at[i])
        for i, (source, target) in enumerate(
            [
                (key_weight_ref.at[0, pl.ds(feature, SLICE)], key_weight),
                (value_weight_ref.at[0, pl.ds(feature, SLICE)], value_weight),
                (cot_ref.at[0, sample, zq], cot),
                (out_ref.at[0, sample, zq], out),
                (query_ref.at[0, sample, zq], query),
            ]
        )
    ]
    for copy in copies:
        copy.start()
    copies[0].wait()
    copies[1].wait()
    for g in range(KVH):
        weight_ref[:, 2 * g * HD : (2 * g + 1) * HD] = key_weight[:, g * HD : (g + 1) * HD]
        weight_ref[:, (2 * g + 1) * HD : (2 * g + 2) * HD] = value_weight[:, g * HD : (g + 1) * HD]

    head = lax.broadcasted_iota(jnp.int32, (4, HD), 0) == zq
    place = lax.broadcasted_iota(jnp.int32, (TXT, HD), 0)
    lane = lax.broadcasted_iota(jnp.int32, (TXT, HD), 1)
    twice = jnp.where(lane % TXT == place, 1.0, 0.0).astype(jnp.bfloat16)
    norms = lax.dot_general(norm_ref[0, sample], twice, NN, preferred_element_type=jnp.float32)
    norm = jnp.sum(jnp.where(head, norms, 0.0), axis=0, keepdims=True)

    copies[2].wait()
    row_mask = jnp.where(place < length_ref[sample], 1.0, 0.0)
    gate = jnp.tanh(jnp.full((TXT, HD), gate_ref[0], jnp.float32))
    scaled = (gate * cot[...].astype(jnp.float32) * row_mask).astype(jnp.bfloat16)
    pack_ref[TXT : 2 * TXT] = scaled
    copies[3].wait()
    product = scaled.astype(jnp.float32) * out[...].astype(jnp.float32)
    product = jnp.concatenate([product, product], axis=0)
    delta = jnp.sum(product.T, axis=0, keepdims=True)
    row = lax.broadcasted_iota(jnp.int32, (16, HD), 0)
    pack_ref[META : META + 16] = jnp.where(
        row == 0, norm, jnp.where(row == 1, delta, 0.0)
    ).astype(jnp.bfloat16)
    copies[4].wait()
    pack_ref[0:TXT] = query[...]


def prepare(layer_gate, text_lens, query, out, cot, norm, key_weight, value_weight):
    whole = pl.BlockSpec(memory_space=pl.ANY)
    vmem = pl.BlockSpec(memory_space=pltpu.VMEM)
    smem = pl.BlockSpec(memory_space=pltpu.SMEM)
    head = pltpu.VMEM((TXT, HD), jnp.bfloat16)
    rows = pltpu.VMEM((SLICE, KVH * HD), jnp.bfloat16)
    return pl.pallas_call(
        prepare_kernel,
        in_specs=[smem, smem, whole, whole, whole, vmem, whole, whole],
        out_specs=[vmem, vmem],
        out_shape=[
            jax.ShapeDtypeStruct((PACK, HD), jnp.bfloat16),
            jax.ShapeDtypeStruct((SLICE, 2 * KVH * HD), jnp.bfloat16),
        ],
        scratch_shapes=[head, head, head, rows, rows, pltpu.SemaphoreType.DMA((5,))],
        compiler_params=pltpu.CompilerParams(vmem_limit_bytes=VMEM_LIMIT),
        cost_estimate=pl.CostEstimate(flops=1 << 16, bytes_accessed=1 << 18, transcendentals=8192),
    )(layer_gate, text_lens, query, out, cot, norm, key_weight, value_weight)


def attention_kernel(tiles_ref, pack_ref, key_ref, value_ref, out_ref):
    rows = key_ref.shape[0]
    x, zb, zq, zh, y = (lax.axis_index(name) for name in ("x", "zb", "zq", "zh", "y"))
    tiles = tiles_ref[x * 2 + zb]
    row = lax.broadcasted_iota(jnp.int32, (rows, GROUP), 0)
    position = (zq * 16 + zh * 4 + y) * ROWS + row
    second = position >= TILE_PAD
    inside = jnp.where(second, position - TILE_PAD, position) < TILE_LEN
    present = jnp.where(second, 1, 0) < tiles
    mask = jnp.where(inside & present & (row < ROWS), 1.0, 0.0)

    query = pack_ref[:, :, 0, 0:TXT, :].reshape(GROUP, HD)
    grad = pack_ref[:, :, 0, TXT : 2 * TXT, :].reshape(GROUP, HD)
    meta = pack_ref[:, :, 0, META : META + 16, :].astype(jnp.float32)
    left = lax.broadcasted_iota(jnp.int32, (1, HD), 1) < TXT

    def line(which):
        picked = [meta[i // 4, i % 4, which : which + 1] for i in range(8)]
        return jnp.concatenate(
            [jnp.where(left, picked[i], picked[i + 1]) for i in range(0, 8, 2)], axis=1
        )

    scores = lax.dot_general(key_ref[...], query, NT, preferred_element_type=jnp.float32) * SCALING
    attention = jnp.exp(scores - line(0)) * mask
    value_grad = lax.dot_general(
        attention.astype(jnp.bfloat16), grad, NN, preferred_element_type=jnp.float32
    )
    probs = lax.dot_general(value_ref[...], grad, NT, preferred_element_type=jnp.float32)
    grad_scores = (attention * (probs - line(1))).astype(jnp.bfloat16)
    key_grad = lax.dot_general(grad_scores, query, NN, preferred_element_type=jnp.float32) * SCALING
    out_ref[:, 0:HD] = key_grad.astype(jnp.bfloat16)
    out_ref[:, HD : 2 * HD] = value_grad.astype(jnp.bfloat16)


def attention_grads(tiles, packed, keys, values):
    rows = keys.shape[0]
    head = pl.BlockSpec((rows, HD), lambda g: (0, g))
    return pl.pallas_call(
        attention_kernel,
        grid=(KVH,),
        in_specs=[
            pl.BlockSpec(memory_space=pltpu.SMEM),
            pl.BlockSpec((2, 4, 1, PACK, HD), lambda g: (g % 2, 0, g // 2, 0, 0)),
            head,
            head,
        ],
        out_specs=pl.BlockSpec((rows, 2 * HD), lambda g: (0, g)),
        out_shape=jax.ShapeDtypeStruct((rows, 2 * KVH * HD), jnp.bfloat16),
        compiler_params=pltpu.CompilerParams(vmem_limit_bytes=VMEM_LIMIT),
        cost_estimate=pl.CostEstimate(
            flops=8 * rows * KVH * GROUP * HD,
            bytes_accessed=3 << 20,
            transcendentals=rows * KVH * GROUP,
        ),
    )(tiles, packed, keys, values)


def to_all(array, axes, count):
    copies = jnp.broadcast_to(array[None], (count, *array.shape))
    return lax.all_to_all(copies, axes, split_axis=0, concat_axis=0, tiled=True)


def body(
    text_query,
    attn_out,
    grad_out,
    log_norm,
    image_keys,
    image_values,
    k_weight,
    v_weight,
    layer_gate,
    tile_counts,
    text_lens,
):
    rows = image_keys.shape[1]
    padded = -(-rows // 8) * 8
    packed, weight = prepare(
        layer_gate, text_lens, text_query, attn_out, grad_out, log_norm, k_weight, v_weight
    )
    weight = lax.all_gather(weight, ("zh", "zb", "zq"), axis=0, tiled=True)

    keys = jnp.pad(image_keys[0], ((0, padded - rows), (0, 0)))
    values = jnp.pad(image_values[0], ((0, padded - rows), (0, 0)))

    def attend(packed):
        packed = lax.all_gather(packed, "zh", axis=0, tiled=False)
        packed = to_all(packed, "zq", 4)
        packed = to_all(packed, "y", 4)
        return attention_grads(tile_counts, packed, keys, values)

    both = lax.cond(
        jnp.max(text_lens) > 0,
        attend,
        lambda _: jnp.zeros((padded, 2 * KVH * HD), jnp.bfloat16),
        packed,
    )

    both = to_all(both, ("x", "y"), 16).reshape(16 * padded, 2 * KVH * HD)
    halves = weight.reshape(2, 256, 2 * KVH * HD)
    part = jnp.stack(
        [
            lax.dot_general(both, halves[t], NT, preferred_element_type=jnp.float32).astype(
                jnp.bfloat16
            )
            for t in range(2)
        ]
    )
    part = part.reshape(32, padded, 256)
    part = lax.all_to_all(part, ("core", "x", "y"), split_axis=0, concat_axis=0, tiled=True)
    part = part.reshape(2, 4, 4, padded, 2, HD).astype(jnp.float32)
    total = (part[0] + part[1])[:, :, :rows]
    return total.transpose(2, 3, 1, 0, 4).reshape(rows, 2 * 4 * 4 * HD)


def solution(mesh):
    fine = Mesh(mesh.devices.reshape(SIZES), NAMES)
    tensor = ("zh", "y")
    rows = ("x", "zb", "zq", "zh", "y")
    in_specs = (
        P("core", None, tensor, None, None),
        P("core", None, tensor, None, None),
        P("core", None, tensor, None, None),
        P("core", None, tensor, None),
        P("core", rows, None),
        P("core", rows, None),
        P("core", tensor, None),
        P("core", tensor, None),
        P("core"),
        P(),
        P(),
    )
    return jax.shard_map(
        body, mesh=fine, in_specs=in_specs, out_specs=P(rows, "core"), check_vma=False
    )
```

```python
import math

import jax
import jax.numpy as jnp
from jax import lax
from jax.experimental import pallas as pl
from jax.experimental.pallas import tpu as pltpu
from jax.sharding import Mesh, PartitionSpec as P

KVH = 8
HD = 128
TXT = 64
TILE_LEN = 1601
TILE_PAD = 1664
NAMES = ("core", "x", "zb", "z1", "z0", "zh", "y")
SIZES = (2, 4, 2, 2, 2, 4, 4)
SCALING = 1.0 / math.sqrt(HD)
META = 2 * TXT
PACK = META + 16
ROWS = 52
PADDED = 56
GROUP = 4 * TXT
SLICE = 32
NT = (((1,), (1,)), ((), ()))
NN = (((1,), (0,)), ((), ()))
VMEM_LIMIT = 16 * 1024 * 1024


def prepare_kernel(
    gate_ref,
    length_ref,
    query_ref,
    out_ref,
    cot_ref,
    norm_ref,
    key_weight_ref,
    value_weight_ref,
    pack_ref,
    weight_ref,
    query,
    out,
    cot,
    key_weight,
    value_weight,
    sems,
):
    x, zb, z1, z0 = (lax.axis_index(name) for name in ("x", "zb", "z1", "z0"))
    zq = z1 * 2 + z0
    sample = x * 2 + zb
    feature = pl.multiple_of(x * 128 + (zb * 2 + z1) * SLICE, SLICE)
    copies = [
        pltpu.make_async_copy(source, target, sems.at[i])
        for i, (source, target) in enumerate(
            [
                (key_weight_ref.at[0, pl.ds(feature, SLICE)], key_weight),
                (value_weight_ref.at[0, pl.ds(feature, SLICE)], value_weight),
                (cot_ref.at[0, sample, zq], cot),
                (out_ref.at[0, sample, zq], out),
                (query_ref.at[0, sample, zq], query),
            ]
        )
    ]
    for copy in copies:
        copy.start()
    copies[0].wait()
    copies[1].wait()
    for g in range(KVH):
        place = 2 * (g % 2 * 4 + g // 2) * HD
        weight_ref[:, place : place + HD] = key_weight[:, g * HD : (g + 1) * HD]
        weight_ref[:, place + HD : place + 2 * HD] = value_weight[:, g * HD : (g + 1) * HD]

    head = lax.broadcasted_iota(jnp.int32, (4, HD), 0) == zq
    place = lax.broadcasted_iota(jnp.int32, (TXT, HD), 0)
    lane = lax.broadcasted_iota(jnp.int32, (TXT, HD), 1)
    twice = jnp.where(lane % TXT == place, 1.0, 0.0).astype(jnp.bfloat16)
    norms = lax.dot_general(norm_ref[0, sample], twice, NN, preferred_element_type=jnp.float32)
    norm = jnp.sum(jnp.where(head, norms, 0.0), axis=0, keepdims=True)

    copies[2].wait()
    row_mask = jnp.where(place < length_ref[sample], 1.0, 0.0)
    gate = jnp.tanh(jnp.full((TXT, HD), gate_ref[0], jnp.float32))
    scaled = (gate * cot[...].astype(jnp.float32) * row_mask).astype(jnp.bfloat16)
    pack_ref[TXT : 2 * TXT] = scaled
    copies[3].wait()
    product = scaled.astype(jnp.float32) * out[...].astype(jnp.float32)
    product = jnp.concatenate([product, product], axis=0)
    delta = jnp.sum(product.T, axis=0, keepdims=True)
    row = lax.broadcasted_iota(jnp.int32, (16, HD), 0)
    pack_ref[META : META + 16] = jnp.where(
        row == 0, norm, jnp.where(row == 1, delta, 0.0)
    ).astype(jnp.bfloat16)
    copies[4].wait()
    pack_ref[0:TXT] = query[...]


def prepare(layer_gate, text_lens, query, out, cot, norm, key_weight, value_weight):
    whole = pl.BlockSpec(memory_space=pltpu.HBM)
    vmem = pl.BlockSpec(memory_space=pltpu.VMEM)
    smem = pl.BlockSpec(memory_space=pltpu.SMEM)
    head = pltpu.VMEM((TXT, HD), jnp.bfloat16)
    rows = pltpu.VMEM((SLICE, KVH * HD), jnp.bfloat16)
    return pl.pallas_call(
        prepare_kernel,
        in_specs=[smem, smem, whole, whole, whole, vmem, whole, whole],
        out_specs=[vmem, vmem],
        out_shape=[
            jax.ShapeDtypeStruct((PACK, HD), jnp.bfloat16),
            jax.ShapeDtypeStruct((SLICE, 2 * KVH * HD), jnp.bfloat16),
        ],
        scratch_shapes=[head, head, head, rows, rows, pltpu.SemaphoreType.DMA((5,))],
        compiler_params=pltpu.CompilerParams(vmem_limit_bytes=VMEM_LIMIT),
        cost_estimate=pl.CostEstimate(flops=1 << 16, bytes_accessed=1 << 18, transcendentals=8192),
    )(layer_gate, text_lens, query, out, cot, norm, key_weight, value_weight)


def split_heads_kernel(key_ref, value_ref, out_ref):
    below = jnp.zeros((PADDED - ROWS, HD), jnp.float32)
    for part, ref in enumerate((key_ref, value_ref)):
        for g in range(KVH):
            head = ref[0, :, g * HD : (g + 1) * HD].astype(jnp.float32)
            head = jnp.concatenate([head, below], axis=0).astype(jnp.bfloat16)
            place = (g // 2 * 2 + part) * HD
            out_ref[g % 2 * 2, :, place : place + HD] = head
            out_ref[g % 2 * 2 + 1, :, place : place + HD] = head


def split_heads(keys, values):
    return pl.pallas_call(
        split_heads_kernel,
        out_shape=jax.ShapeDtypeStruct((4, PADDED, KVH * HD), jnp.bfloat16),
        compiler_params=pltpu.CompilerParams(vmem_limit_bytes=VMEM_LIMIT),
        cost_estimate=pl.CostEstimate(flops=0, bytes_accessed=700000, transcendentals=0),
    )(keys, values)


def attention_kernel(block_ref, tiles_ref, pack_ref, heads_ref, out_ref):
    del block_ref
    x, zb, z1, z0, zh = (lax.axis_index(name) for name in ("x", "zb", "z1", "z0", "zh"))
    tiles = tiles_ref[x * 2 + zb]
    query = pack_ref[:, 0, 0:TXT, :].reshape(GROUP, HD)
    grad = pack_ref[:, 0, TXT : 2 * TXT, :].reshape(GROUP, HD)
    meta = pack_ref[:, 0, META : META + 16, :].astype(jnp.float32)
    left = lax.broadcasted_iota(jnp.int32, (1, HD), 1) < TXT

    def line(which):
        picked = [meta[i, which : which + 1] for i in range(4)]
        return jnp.concatenate(
            [jnp.where(left, picked[i], picked[i + 1]) for i in range(0, 4, 2)], axis=1
        )

    norm, delta = line(0), line(1)
    row = lax.broadcasted_iota(jnp.int32, (PADDED, GROUP), 0)
    for y in range(4):
        position = ((z1 * 2 + z0) * 16 + zh * 4 + y) * ROWS + row
        second = position >= TILE_PAD
        inside = jnp.where(second, position - TILE_PAD, position) < TILE_LEN
        present = jnp.where(second, 1, 0) < tiles
        mask = jnp.where(inside & present & (row < ROWS), 1.0, 0.0)
        keys = heads_ref[y, :, 0:HD]
        values = heads_ref[y, :, HD : 2 * HD]
        scores = lax.dot_general(keys, query, NT, preferred_element_type=jnp.float32) * SCALING
        attention = jnp.exp(scores - norm) * mask
        value_grad = lax.dot_general(
            attention.astype(jnp.bfloat16), grad, NN, preferred_element_type=jnp.float32
        )
        probs = lax.dot_general(values, grad, NT, preferred_element_type=jnp.float32)
        grad_scores = (attention * (probs - delta)).astype(jnp.bfloat16)
        key_grad = lax.dot_general(grad_scores, query, NN, preferred_element_type=jnp.float32)
        out_ref[y, :, 0:HD] = (key_grad * SCALING).astype(jnp.bfloat16)
        out_ref[y, :, HD : 2 * HD] = value_grad.astype(jnp.bfloat16)


def attention_grads(block, tiles, packed, heads):
    piece = pl.BlockSpec((4, PADDED, 2 * HD), lambda s, b: (0, 0, (b[0] + 4 - s) % 4))
    return pl.pallas_call(
        attention_kernel,
        grid_spec=pltpu.PrefetchScalarGridSpec(
            num_scalar_prefetch=1,
            grid=(4,),
            in_specs=[
                pl.BlockSpec(memory_space=pltpu.SMEM),
                pl.BlockSpec((4, 1, PACK, HD), lambda s, b: (0, s, 0, 0)),
                piece,
            ],
            out_specs=piece,
        ),
        out_shape=jax.ShapeDtypeStruct((4, PADDED, KVH * HD), jnp.bfloat16),
        compiler_params=pltpu.CompilerParams(vmem_limit_bytes=VMEM_LIMIT),
        cost_estimate=pl.CostEstimate(
            flops=8 * 4 * PADDED * 4 * GROUP * HD,
            bytes_accessed=2 << 20,
            transcendentals=4 * PADDED * 4 * GROUP,
        ),
    )(block, tiles, packed, heads)


def project_kernel(grads_ref, weight_ref, out_ref):
    wide = KVH * HD
    for t in range(2):
        for h in range(2):
            rows = slice(h * 2 * PADDED, (h + 1) * 2 * PADDED)
            total = sum(
                lax.dot_general(
                    grads_ref[0, 2 * p + h],
                    weight_ref[t * 256 : (t + 1) * 256, p * wide : (p + 1) * wide],
                    NT,
                    preferred_element_type=jnp.float32,
                )
                for p in range(2)
            )
            out_ref[t, 0, rows] = total.astype(jnp.bfloat16)


def project(grads, weight):
    features, depth = weight.shape
    rows = 4 * PADDED
    return pl.pallas_call(
        project_kernel,
        grid=(4,),
        in_specs=[
            pl.BlockSpec((1, 4, rows // 2, depth // 2), lambda x: (x, 0, 0, 0)),
            pl.BlockSpec((features, depth), lambda x: (0, 0)),
        ],
        out_specs=pl.BlockSpec((2, 1, rows, features // 2), lambda x: (0, x, 0, 0)),
        out_shape=jax.ShapeDtypeStruct((2, 4, rows, features // 2), jnp.bfloat16),
        compiler_params=pltpu.CompilerParams(vmem_limit_bytes=VMEM_LIMIT),
        cost_estimate=pl.CostEstimate(
            flops=8 * rows * features * depth, bytes_accessed=7 << 20, transcendentals=0
        ),
    )(grads, weight)


def to_all(array, axes, count):
    copies = jnp.broadcast_to(array[None], (count, *array.shape))
    return lax.all_to_all(copies, axes, split_axis=0, concat_axis=0, tiled=True)


def body(
    text_query,
    attn_out,
    grad_out,
    log_norm,
    image_keys,
    image_values,
    k_weight,
    v_weight,
    layer_gate,
    tile_counts,
    text_lens,
):
    packed, weight = prepare(
        layer_gate, text_lens, text_query, attn_out, grad_out, log_norm, k_weight, v_weight
    )
    weight = lax.all_gather(weight, ("zh", "zb", "z1"), axis=0, tiled=True)
    zh = lax.axis_index("zh").astype(jnp.int32).reshape(1)
    own = lax.axis_index("y") % 2

    def attend(packed):
        heads = split_heads(image_keys, image_values)
        heads = lax.all_to_all(heads, "y", split_axis=0, concat_axis=0, tiled=True)
        pieces = [packed] + [
            lax.ppermute(packed, "zh", [(i, (i + shift) % 4) for i in range(4)])
            for shift in (1, 2, 3)
        ]
        packed = to_all(jnp.stack(pieces), ("z1", "z0"), 4)
        part = attention_grads(zh, tile_counts, packed, heads)
        part = part.reshape(2, 2 * PADDED, KVH * HD)
        kept = lax.dynamic_index_in_dim(part, own, 0, keepdims=False)
        given = lax.dynamic_index_in_dim(part, 1 - own, 0, keepdims=False)
        taken = lax.ppermute(given, "y", [(0, 1), (1, 0), (2, 3), (3, 2)])
        return (kept.astype(jnp.float32) + taken.astype(jnp.float32)).astype(jnp.bfloat16)

    grads = lax.cond(
        jnp.max(text_lens) > 0,
        attend,
        lambda _: jnp.zeros((2 * PADDED, KVH * HD), jnp.bfloat16),
        packed,
    )

    grads = to_all(grads, ("x", "y"), 16).reshape(4, 4, 2 * PADDED, KVH * HD)
    part = project(grads, weight).reshape(32, PADDED, 256)
    part = lax.all_to_all(part, ("core", "x", "y"), split_axis=0, concat_axis=0, tiled=True)
    part = part.reshape(2, 4, 4, PADDED, 2, HD).astype(jnp.float32)
    total = (part[0] + part[1])[:, :, :ROWS]
    return total.transpose(2, 3, 1, 0, 4).reshape(ROWS, 2 * 4 * 4 * HD)


def solution(mesh):
    fine = Mesh(mesh.devices.reshape(SIZES), NAMES)
    tensor = ("zh", "y")
    rows = ("x", "zb", "z1", "z0", "zh", "y")
    in_specs = (
        P("core", None, tensor, None, None),
        P("core", None, tensor, None, None),
        P("core", None, tensor, None, None),
        P("core", None, tensor, None),
        P("core", rows, None),
        P("core", rows, None),
        P("core", tensor, None),
        P("core", tensor, None),
        P("core"),
        P(),
        P(),
    )
    return jax.shard_map(
        body, mesh=fine, in_specs=in_specs, out_specs=P(rows, "core"), check_vma=False
    )
```

```python
import math

import jax
import jax.numpy as jnp
from jax import lax
from jax.experimental import pallas as pl
from jax.experimental.pallas import tpu as pltpu
from jax.sharding import Mesh, PartitionSpec as P

KVH = 8
HD = 128
TXT = 64
TILE_LEN = 1601
TILE_PAD = 1664
NAMES = ("core", "x", "zb", "z1", "z0", "zh", "y")
SIZES = (2, 4, 2, 2, 2, 4, 4)
SCALING = 1.0 / math.sqrt(HD)
META = 2 * TXT
PACK = META + 16
ROWS = 52
PADDED = 56
GROUP = 4 * TXT
SLICE = 32
NT = (((1,), (1,)), ((), ()))
NN = (((1,), (0,)), ((), ()))
VMEM_LIMIT = 16 * 1024 * 1024
WHOLE_VMEM = 60 * 1024 * 1024


def prepare_kernel(
    gate_ref,
    length_ref,
    query_ref,
    out_ref,
    cot_ref,
    norm_ref,
    key_weight_ref,
    value_weight_ref,
    pack_ref,
    weight_ref,
    query,
    out,
    cot,
    key_weight,
    value_weight,
    sems,
):
    x, zb, z1, z0 = (lax.axis_index(name) for name in ("x", "zb", "z1", "z0"))
    zq = z1 * 2 + z0
    sample = x * 2 + zb
    feature = pl.multiple_of(x * 128 + (zb * 2 + z1) * SLICE, SLICE)
    copies = [
        pltpu.make_async_copy(source, target, sems.at[i])
        for i, (source, target) in enumerate(
            [
                (key_weight_ref.at[0, pl.ds(feature, SLICE)], key_weight),
                (value_weight_ref.at[0, pl.ds(feature, SLICE)], value_weight),
                (cot_ref.at[0, sample, zq], cot),
                (out_ref.at[0, sample, zq], out),
                (query_ref.at[0, sample, zq], query),
            ]
        )
    ]
    for copy in copies:
        copy.start()
    copies[0].wait()
    copies[1].wait()
    for g in range(KVH):
        place = 2 * (g % 2 * 4 + g // 2) * HD
        weight_ref[:, place : place + HD] = key_weight[:, g * HD : (g + 1) * HD]
        weight_ref[:, place + HD : place + 2 * HD] = value_weight[:, g * HD : (g + 1) * HD]

    head = lax.broadcasted_iota(jnp.int32, (4, HD), 0) == zq
    place = lax.broadcasted_iota(jnp.int32, (TXT, HD), 0)
    lane = lax.broadcasted_iota(jnp.int32, (TXT, HD), 1)
    twice = jnp.where(lane % TXT == place, 1.0, 0.0).astype(jnp.bfloat16)
    norms = lax.dot_general(norm_ref[0, sample], twice, NN, preferred_element_type=jnp.float32)
    norm = jnp.sum(jnp.where(head, norms, 0.0), axis=0, keepdims=True)

    copies[2].wait()
    row_mask = jnp.where(place < length_ref[sample], 1.0, 0.0)
    gate = jnp.tanh(jnp.full((TXT, HD), gate_ref[0], jnp.float32))
    scaled = (gate * cot[...].astype(jnp.float32) * row_mask).astype(jnp.bfloat16)
    pack_ref[TXT : 2 * TXT] = scaled
    copies[3].wait()
    product = scaled.astype(jnp.float32) * out[...].astype(jnp.float32)
    product = jnp.concatenate([product, product], axis=0)
    delta = jnp.sum(product.T, axis=0, keepdims=True)
    row = lax.broadcasted_iota(jnp.int32, (16, HD), 0)
    pack_ref[META : META + 16] = jnp.where(
        row == 0, norm, jnp.where(row == 1, delta, 0.0)
    ).astype(jnp.bfloat16)
    copies[4].wait()
    pack_ref[0:TXT] = query[...]


def prepare(layer_gate, text_lens, query, out, cot, norm, key_weight, value_weight):
    whole = pl.BlockSpec(memory_space=pltpu.HBM)
    vmem = pl.BlockSpec(memory_space=pltpu.VMEM)
    smem = pl.BlockSpec(memory_space=pltpu.SMEM)
    head = pltpu.VMEM((TXT, HD), jnp.bfloat16)
    rows = pltpu.VMEM((SLICE, KVH * HD), jnp.bfloat16)
    return pl.pallas_call(
        prepare_kernel,
        in_specs=[smem, smem, whole, whole, whole, vmem, whole, whole],
        out_specs=[vmem, vmem],
        out_shape=[
            jax.ShapeDtypeStruct((PACK, HD), jnp.bfloat16),
            jax.ShapeDtypeStruct((SLICE, 2 * KVH * HD), jnp.bfloat16),
        ],
        scratch_shapes=[head, head, head, rows, rows, pltpu.SemaphoreType.DMA((5,))],
        compiler_params=pltpu.CompilerParams(vmem_limit_bytes=WHOLE_VMEM),
        cost_estimate=pl.CostEstimate(flops=1 << 16, bytes_accessed=1 << 18, transcendentals=8192),
    )(layer_gate, text_lens, query, out, cot, norm, key_weight, value_weight)


def split_heads_kernel(key_ref, value_ref, out_ref):
    below = jnp.zeros((PADDED - ROWS, HD), jnp.float32)
    for part, ref in enumerate((key_ref, value_ref)):
        for g in range(KVH):
            head = ref[0, :, g * HD : (g + 1) * HD].astype(jnp.float32)
            head = jnp.concatenate([head, below], axis=0).astype(jnp.bfloat16)
            place = (g // 2 * 2 + part) * HD
            out_ref[g % 2 * 2, :, place : place + HD] = head
            out_ref[g % 2 * 2 + 1, :, place : place + HD] = head


def split_heads(keys, values):
    return pl.pallas_call(
        split_heads_kernel,
        out_shape=jax.ShapeDtypeStruct((4, PADDED, KVH * HD), jnp.bfloat16),
        compiler_params=pltpu.CompilerParams(vmem_limit_bytes=VMEM_LIMIT),
        cost_estimate=pl.CostEstimate(flops=0, bytes_accessed=700000, transcendentals=0),
    )(keys, values)


def attention_kernel(tiles_ref, pack_ref, heads_ref, out_ref):
    x, zb, z1, z0, zh = (lax.axis_index(name) for name in ("x", "zb", "z1", "z0", "zh"))
    tiles = tiles_ref[x * 2 + zb]
    query = pack_ref[:, 0, 0:TXT, :].reshape(GROUP, HD)
    grad = pack_ref[:, 0, TXT : 2 * TXT, :].reshape(GROUP, HD)
    meta = pack_ref[:, 0, META : META + 16, :].astype(jnp.float32)
    left = lax.broadcasted_iota(jnp.int32, (1, HD), 1) < TXT

    def line(which):
        picked = [meta[i, which : which + 1] for i in range(4)]
        return jnp.concatenate(
            [jnp.where(left, picked[i], picked[i + 1]) for i in range(0, 4, 2)], axis=1
        )

    norm, delta = line(0), line(1)
    row = lax.broadcasted_iota(jnp.int32, (PADDED, GROUP), 0)
    for y in range(4):
        position = ((z1 * 2 + z0) * 16 + zh * 4 + y) * ROWS + row
        second = position >= TILE_PAD
        inside = jnp.where(second, position - TILE_PAD, position) < TILE_LEN
        present = jnp.where(second, 1, 0) < tiles
        mask = jnp.where(inside & present & (row < ROWS), 1.0, 0.0)
        keys = heads_ref[y, :, 0:HD]
        values = heads_ref[y, :, HD : 2 * HD]
        scores = lax.dot_general(keys, query, NT, preferred_element_type=jnp.float32) * SCALING
        attention = jnp.exp(scores - norm) * mask
        value_grad = lax.dot_general(
            attention.astype(jnp.bfloat16), grad, NN, preferred_element_type=jnp.float32
        )
        probs = lax.dot_general(values, grad, NT, preferred_element_type=jnp.float32)
        grad_scores = (attention * (probs - delta)).astype(jnp.bfloat16)
        key_grad = lax.dot_general(grad_scores, query, NN, preferred_element_type=jnp.float32)
        out_ref[y, :, 0:HD] = (key_grad * SCALING).astype(jnp.bfloat16)
        out_ref[y, :, HD : 2 * HD] = value_grad.astype(jnp.bfloat16)


def attention_grads(tiles, packed, heads):
    piece = pl.BlockSpec((4, PADDED, 2 * HD), lambda s: (0, 0, s))
    return pl.pallas_call(
        attention_kernel,
        grid=(4,),
        in_specs=[
            pl.BlockSpec(memory_space=pltpu.SMEM),
            pl.BlockSpec((4, 1, PACK, HD), lambda s: (0, s, 0, 0)),
            piece,
        ],
        out_specs=piece,
        out_shape=jax.ShapeDtypeStruct((4, PADDED, KVH * HD), jnp.bfloat16),
        compiler_params=pltpu.CompilerParams(vmem_limit_bytes=VMEM_LIMIT),
        cost_estimate=pl.CostEstimate(
            flops=8 * 4 * PADDED * 4 * GROUP * HD,
            bytes_accessed=2 << 20,
            transcendentals=4 * PADDED * 4 * GROUP,
        ),
    )(tiles, packed, heads)


def project_kernel(grads_ref, weight_ref, out_ref):
    wide = KVH * HD
    for t in range(2):
        for h in range(2):
            rows = slice(h * 2 * PADDED, (h + 1) * 2 * PADDED)
            total = sum(
                lax.dot_general(
                    grads_ref[0, 2 * p + h],
                    weight_ref[t * 256 : (t + 1) * 256, p * wide : (p + 1) * wide],
                    NT,
                    preferred_element_type=jnp.float32,
                )
                for p in range(2)
            )
            out_ref[t, 0, rows] = total.astype(jnp.bfloat16)


def project(grads, weight):
    features, depth = weight.shape
    rows = 4 * PADDED
    return pl.pallas_call(
        project_kernel,
        grid=(4,),
        in_specs=[
            pl.BlockSpec((1, 4, rows // 2, depth // 2), lambda x: (x, 0, 0, 0)),
            pl.BlockSpec((features, depth), lambda x: (0, 0)),
        ],
        out_specs=pl.BlockSpec((2, 1, rows, features // 2), lambda x: (0, x, 0, 0)),
        out_shape=jax.ShapeDtypeStruct((2, 4, rows, features // 2), jnp.bfloat16),
        compiler_params=pltpu.CompilerParams(vmem_limit_bytes=WHOLE_VMEM),
        cost_estimate=pl.CostEstimate(
            flops=8 * rows * features * depth, bytes_accessed=7 << 20, transcendentals=0
        ),
    )(grads, weight)


def to_all(array, axes, count):
    copies = jnp.broadcast_to(array[None], (count, *array.shape))
    return lax.all_to_all(copies, axes, split_axis=0, concat_axis=0, tiled=True)


def body(
    text_query,
    attn_out,
    grad_out,
    log_norm,
    image_keys,
    image_values,
    k_weight,
    v_weight,
    layer_gate,
    tile_counts,
    text_lens,
):
    packed, weight = prepare(
        layer_gate, text_lens, text_query, attn_out, grad_out, log_norm, k_weight, v_weight
    )
    weight = lax.all_gather(weight, ("zh", "zb", "z1"), axis=0, tiled=True)
    own = lax.axis_index("y") % 2

    def attend(packed):
        heads = split_heads(image_keys, image_values)
        heads = lax.all_to_all(heads, "y", split_axis=0, concat_axis=0, tiled=True)
        packed = lax.all_gather(packed, "zh", axis=0, tiled=True)
        packed = to_all(packed, ("z1", "z0"), 4).reshape(4, 4, PACK, HD)
        part = attention_grads(tile_counts, packed, heads)
        part = part.reshape(2, 2 * PADDED, KVH * HD)
        kept = lax.dynamic_index_in_dim(part, own, 0, keepdims=False)
        given = lax.dynamic_index_in_dim(part, 1 - own, 0, keepdims=False)
        taken = lax.ppermute(given, "y", [(0, 1), (1, 0), (2, 3), (3, 2)])
        return (kept.astype(jnp.float32) + taken.astype(jnp.float32)).astype(jnp.bfloat16)

    grads = lax.cond(
        jnp.max(text_lens) > 0,
        attend,
        lambda _: jnp.zeros((2 * PADDED, KVH * HD), jnp.bfloat16),
        packed,
    )

    grads = to_all(grads, ("x", "y"), 16).reshape(4, 4, 2 * PADDED, KVH * HD)
    part = project(grads, weight).reshape(32, PADDED, 256)
    part = lax.all_to_all(part, ("core", "x", "y"), split_axis=0, concat_axis=0, tiled=True)
    part = part.reshape(2, 4, 4, PADDED, 2, HD).astype(jnp.float32)
    total = (part[0] + part[1])[:, :, :ROWS]
    return total.transpose(2, 3, 1, 0, 4).reshape(ROWS, 2 * 4 * 4 * HD)


def solution(mesh):
    fine = Mesh(mesh.devices.reshape(SIZES), NAMES)
    tensor = ("zh", "y")
    rows = ("x", "zb", "z1", "z0", "zh", "y")
    in_specs = (
        P("core", None, tensor, None, None),
        P("core", None, tensor, None, None),
        P("core", None, tensor, None, None),
        P("core", None, tensor, None),
        P("core", rows, None),
        P("core", rows, None),
        P("core", tensor, None),
        P("core", tensor, None),
        P("core"),
        P(),
        P(),
    )
    return jax.shard_map(
        body, mesh=fine, in_specs=in_specs, out_specs=P(rows, "core"), check_vma=False
    )
```

```python
import math

import jax
import jax.numpy as jnp
from jax import lax
from jax.experimental import pallas as pl
from jax.experimental.pallas import tpu as pltpu
from jax.sharding import Mesh, PartitionSpec as P

KVH = 8
HD = 128
TXT = 64
TILE_LEN = 1601
TILE_PAD = 1664
NAMES = ("core", "x", "zb", "z1", "z0", "zh", "y")
SIZES = (2, 4, 2, 2, 2, 4, 4)
SCALING = 1.0 / math.sqrt(HD)
META = 2 * TXT
PACK = META + 16
ROWS = 52
PADDED = 56
GROUP = 4 * TXT
SLICE = 32
NT = (((1,), (1,)), ((), ()))
NN = (((1,), (0,)), ((), ()))
VMEM_LIMIT = 16 * 1024 * 1024
WHOLE_VMEM = 60 * 1024 * 1024


def prepare_kernel(
    gate_ref,
    length_ref,
    query_ref,
    out_ref,
    cot_ref,
    norm_ref,
    key_weight_ref,
    value_weight_ref,
    pack_ref,
    weight_ref,
    longest_ref,
    query,
    out,
    cot,
    key_weight,
    value_weight,
    sems,
):
    x, zb, z1, z0 = (lax.axis_index(name) for name in ("x", "zb", "z1", "z0"))
    zq = z1 * 2 + z0
    sample = x * 2 + zb
    feature = pl.multiple_of(x * 128 + (zb * 2 + z1) * SLICE, SLICE)
    copies = [
        pltpu.make_async_copy(source, target, sems.at[i])
        for i, (source, target) in enumerate(
            [
                (key_weight_ref.at[0, pl.ds(feature, SLICE)], key_weight),
                (value_weight_ref.at[0, pl.ds(feature, SLICE)], value_weight),
                (cot_ref.at[0, sample, zq], cot),
                (out_ref.at[0, sample, zq], out),
                (query_ref.at[0, sample, zq], query),
            ]
        )
    ]
    for copy in copies:
        copy.start()
    longest = length_ref[0]
    for i in range(1, 8):
        longest = jnp.maximum(longest, length_ref[i])
    longest_ref[0] = longest
    copies[0].wait()
    copies[1].wait()
    for g in range(KVH):
        place = 2 * (g % 2 * 4 + g // 2) * HD
        weight_ref[:, place : place + HD] = key_weight[:, g * HD : (g + 1) * HD]
        weight_ref[:, place + HD : place + 2 * HD] = value_weight[:, g * HD : (g + 1) * HD]

    head = lax.broadcasted_iota(jnp.int32, (4, HD), 0) == zq
    place = lax.broadcasted_iota(jnp.int32, (TXT, HD), 0)
    lane = lax.broadcasted_iota(jnp.int32, (TXT, HD), 1)
    twice = jnp.where(lane % TXT == place, 1.0, 0.0).astype(jnp.bfloat16)
    norms = lax.dot_general(norm_ref[0, sample], twice, NN, preferred_element_type=jnp.float32)
    norm = jnp.sum(jnp.where(head, norms, 0.0), axis=0, keepdims=True)

    copies[2].wait()
    row_mask = jnp.where(place < length_ref[sample], 1.0, 0.0)
    gate = jnp.tanh(jnp.full((TXT, HD), gate_ref[0], jnp.float32))
    scaled = (gate * cot[...].astype(jnp.float32) * row_mask).astype(jnp.bfloat16)
    pack_ref[TXT : 2 * TXT] = scaled
    copies[3].wait()
    product = scaled.astype(jnp.float32) * out[...].astype(jnp.float32)
    product = jnp.concatenate([product, product], axis=0)
    delta = jnp.sum(product.T, axis=0, keepdims=True)
    row = lax.broadcasted_iota(jnp.int32, (16, HD), 0)
    pack_ref[META : META + 16] = jnp.where(
        row == 0, norm, jnp.where(row == 1, delta, 0.0)
    ).astype(jnp.bfloat16)
    copies[4].wait()
    pack_ref[0:TXT] = query[...]


def prepare(layer_gate, text_lens, query, out, cot, norm, key_weight, value_weight):
    whole = pl.BlockSpec(memory_space=pltpu.HBM)
    vmem = pl.BlockSpec(memory_space=pltpu.VMEM)
    smem = pl.BlockSpec(memory_space=pltpu.SMEM)
    head = pltpu.VMEM((TXT, HD), jnp.bfloat16)
    rows = pltpu.VMEM((SLICE, KVH * HD), jnp.bfloat16)
    return pl.pallas_call(
        prepare_kernel,
        in_specs=[smem, smem, whole, whole, whole, vmem, whole, whole],
        out_specs=[vmem, vmem, smem],
        out_shape=[
            jax.ShapeDtypeStruct((PACK, HD), jnp.bfloat16),
            jax.ShapeDtypeStruct((SLICE, 2 * KVH * HD), jnp.bfloat16),
            jax.ShapeDtypeStruct((1,), jnp.int32),
        ],
        scratch_shapes=[head, head, head, rows, rows, pltpu.SemaphoreType.DMA((5,))],
        compiler_params=pltpu.CompilerParams(vmem_limit_bytes=WHOLE_VMEM),
        cost_estimate=pl.CostEstimate(flops=1 << 16, bytes_accessed=1 << 18, transcendentals=8192),
    )(layer_gate, text_lens, query, out, cot, norm, key_weight, value_weight)


def split_heads_kernel(key_ref, value_ref, out_ref):
    below = jnp.zeros((PADDED - ROWS, HD), jnp.float32)
    for part, ref in enumerate((key_ref, value_ref)):
        for g in range(KVH):
            head = ref[0, :, g * HD : (g + 1) * HD].astype(jnp.float32)
            head = jnp.concatenate([head, below], axis=0).astype(jnp.bfloat16)
            place = (g // 2 * 2 + part) * HD
            out_ref[g % 2 * 2, :, place : place + HD] = head
            out_ref[g % 2 * 2 + 1, :, place : place + HD] = head


def split_heads(keys, values):
    return pl.pallas_call(
        split_heads_kernel,
        out_shape=jax.ShapeDtypeStruct((4, PADDED, KVH * HD), jnp.bfloat16),
        compiler_params=pltpu.CompilerParams(vmem_limit_bytes=VMEM_LIMIT),
        cost_estimate=pl.CostEstimate(flops=0, bytes_accessed=700000, transcendentals=0),
    )(keys, values)


def attention_kernel(tiles_ref, pack_ref, heads_ref, out_ref):
    x, zb, z1, z0, zh = (lax.axis_index(name) for name in ("x", "zb", "z1", "z0", "zh"))
    tiles = tiles_ref[x * 2 + zb]
    query = pack_ref[:, 0, 0:TXT, :].reshape(GROUP, HD)
    grad = pack_ref[:, 0, TXT : 2 * TXT, :].reshape(GROUP, HD)
    meta = pack_ref[:, 0, META : META + 16, :].astype(jnp.float32)
    left = lax.broadcasted_iota(jnp.int32, (1, HD), 1) < TXT

    def line(which):
        picked = [meta[i, which : which + 1] for i in range(4)]
        return jnp.concatenate(
            [jnp.where(left, picked[i], picked[i + 1]) for i in range(0, 4, 2)], axis=1
        )

    norm, delta = line(0), line(1)
    line_rows = 4 * PADDED
    wide_row = lax.broadcasted_iota(jnp.int32, (line_rows, GROUP), 0)
    y = sum(jnp.where(wide_row >= i * PADDED, 1, 0) for i in (1, 2, 3))
    row = wide_row - y * PADDED
    position = ((z1 * 2 + z0) * 16 + zh * 4 + y) * ROWS + row
    second = position >= TILE_PAD
    inside = jnp.where(second, position - TILE_PAD, position) < TILE_LEN
    present = jnp.where(second, 1, 0) < tiles
    mask = jnp.where(inside & present & (row < ROWS), 1.0, 0.0)

    def lines(block):
        return block.astype(jnp.float32).reshape(line_rows, HD).astype(jnp.bfloat16)

    keys = lines(heads_ref[:, :, 0:HD])
    values = lines(heads_ref[:, :, HD : 2 * HD])
    scores = lax.dot_general(keys, query, NT, preferred_element_type=jnp.float32) * SCALING
    attention = jnp.exp(scores - norm) * mask
    value_grad = lax.dot_general(
        attention.astype(jnp.bfloat16), grad, NN, preferred_element_type=jnp.float32
    )
    probs = lax.dot_general(values, grad, NT, preferred_element_type=jnp.float32)
    grad_scores = (attention * (probs - delta)).astype(jnp.bfloat16)
    key_grad = lax.dot_general(grad_scores, query, NN, preferred_element_type=jnp.float32) * SCALING
    out_ref[:, :, 0:HD] = key_grad.reshape(4, PADDED, HD).astype(jnp.bfloat16)
    out_ref[:, :, HD : 2 * HD] = value_grad.reshape(4, PADDED, HD).astype(jnp.bfloat16)


def attention_grads(tiles, packed, heads):
    piece = pl.BlockSpec((4, PADDED, 2 * HD), lambda s: (0, 0, s))
    return pl.pallas_call(
        attention_kernel,
        grid=(4,),
        in_specs=[
            pl.BlockSpec(memory_space=pltpu.SMEM),
            pl.BlockSpec((4, 1, PACK, HD), lambda s: (0, s, 0, 0)),
            piece,
        ],
        out_specs=piece,
        out_shape=jax.ShapeDtypeStruct((4, PADDED, KVH * HD), jnp.bfloat16),
        compiler_params=pltpu.CompilerParams(vmem_limit_bytes=VMEM_LIMIT),
        cost_estimate=pl.CostEstimate(
            flops=8 * 4 * PADDED * 4 * GROUP * HD,
            bytes_accessed=2 << 20,
            transcendentals=4 * PADDED * 4 * GROUP,
        ),
    )(tiles, packed, heads)


def project_kernel(grads_ref, weight_ref, out_ref):
    wide = KVH * HD
    total = sum(
        lax.dot_general(
            grads_ref[0, 2 * p : 2 * p + 2].reshape(4 * PADDED, wide),
            weight_ref[:, p * wide : (p + 1) * wide],
            NT,
            preferred_element_type=jnp.float32,
        )
        for p in range(2)
    ).astype(jnp.bfloat16)
    out_ref[0, 0] = total[:, 0:256]
    out_ref[1, 0] = total[:, 256:512]


def project(grads, weight):
    features, depth = weight.shape
    rows = 4 * PADDED
    return pl.pallas_call(
        project_kernel,
        grid=(4,),
        in_specs=[
            pl.BlockSpec((1, 4, rows // 2, depth // 2), lambda x: (x, 0, 0, 0)),
            pl.BlockSpec((features, depth), lambda x: (0, 0)),
        ],
        out_specs=pl.BlockSpec((2, 1, rows, features // 2), lambda x: (0, x, 0, 0)),
        out_shape=jax.ShapeDtypeStruct((2, 4, rows, features // 2), jnp.bfloat16),
        compiler_params=pltpu.CompilerParams(vmem_limit_bytes=WHOLE_VMEM),
        cost_estimate=pl.CostEstimate(
            flops=8 * rows * features * depth, bytes_accessed=7 << 20, transcendentals=0
        ),
    )(grads, weight)


def to_all(array, axes, count):
    copies = jnp.broadcast_to(array[None], (count, *array.shape))
    return lax.all_to_all(copies, axes, split_axis=0, concat_axis=0, tiled=True)


def body(
    text_query,
    attn_out,
    grad_out,
    log_norm,
    image_keys,
    image_values,
    k_weight,
    v_weight,
    layer_gate,
    tile_counts,
    text_lens,
):
    packed, weight, longest = prepare(
        layer_gate, text_lens, text_query, attn_out, grad_out, log_norm, k_weight, v_weight
    )
    weight = lax.all_gather(weight, ("zh", "zb", "z1"), axis=0, tiled=True)
    own = lax.axis_index("y") % 2

    def attend(packed):
        heads = split_heads(image_keys, image_values)
        heads = lax.all_to_all(heads, "y", split_axis=0, concat_axis=0, tiled=True)
        packed = lax.all_gather(packed, "zh", axis=0, tiled=True)
        packed = lax.all_gather(packed, ("z1", "z0"), axis=0, tiled=True)
        packed = packed.reshape(4, 4, PACK, HD)
        part = attention_grads(tile_counts, packed, heads)
        part = part.reshape(2, 2 * PADDED, KVH * HD)
        kept = lax.dynamic_index_in_dim(part, own, 0, keepdims=False)
        given = lax.dynamic_index_in_dim(part, 1 - own, 0, keepdims=False)
        taken = lax.ppermute(given, "y", [(0, 1), (1, 0), (2, 3), (3, 2)])
        return (kept.astype(jnp.float32) + taken.astype(jnp.float32)).astype(jnp.bfloat16)

    grads = lax.cond(
        longest[0] > 0,
        attend,
        lambda _: jnp.zeros((2 * PADDED, KVH * HD), jnp.bfloat16),
        packed,
    )

    grads = to_all(grads, ("x", "y"), 16).reshape(4, 4, 2 * PADDED, KVH * HD)
    part = project(grads, weight).reshape(32, PADDED, 256)
    part = lax.all_to_all(part, ("core", "x", "y"), split_axis=0, concat_axis=0, tiled=True)
    part = part.reshape(2, 4, 4, PADDED, 2, HD).astype(jnp.float32)
    total = (part[0] + part[1])[:, :, :ROWS]
    return total.transpose(2, 3, 1, 0, 4).reshape(ROWS, 2 * 4 * 4 * HD)


def solution(mesh):
    fine = Mesh(mesh.devices.reshape(SIZES), NAMES)
    tensor = ("zh", "y")
    rows = ("x", "zb", "z1", "z0", "zh", "y")
    in_specs = (
        P("core", None, tensor, None, None),
        P("core", None, tensor, None, None),
        P("core", None, tensor, None, None),
        P("core", None, tensor, None),
        P("core", rows, None),
        P("core", rows, None),
        P("core", tensor, None),
        P("core", tensor, None),
        P("core"),
        P(),
        P(),
    )
    return jax.shard_map(
        body, mesh=fine, in_specs=in_specs, out_specs=P(rows, "core"), check_vma=False
    )
```

```python
import math

import jax
import jax.numpy as jnp
from jax import lax
from jax.experimental import pallas as pl
from jax.experimental.pallas import tpu as pltpu
from jax.sharding import Mesh, PartitionSpec as P

KVH = 8
HD = 128
TXT = 64
TILE_LEN = 1601
TILE_PAD = 1664
NAMES = ("core", "x", "zb", "z1", "z0", "zh", "y")
SIZES = (2, 4, 2, 2, 2, 4, 4)
SCALING = 1.0 / math.sqrt(HD)
META = 2 * TXT
PACK = META + 16
ROWS = 52
PADDED = 56
GROUP = 4 * TXT
SLICE = 32
NT = (((1,), (1,)), ((), ()))
NN = (((1,), (0,)), ((), ()))
VMEM_LIMIT = 16 * 1024 * 1024
WHOLE_VMEM = 60 * 1024 * 1024


def prepare_kernel(
    gate_ref,
    length_ref,
    query_ref,
    out_ref,
    cot_ref,
    norm_ref,
    key_weight_ref,
    value_weight_ref,
    pack_ref,
    weight_ref,
    longest_ref,
    query,
    out,
    cot,
    key_weight,
    value_weight,
    sems,
):
    x, zb, z1, z0 = (lax.axis_index(name) for name in ("x", "zb", "z1", "z0"))
    heads = pl.ds(2 * z0, 2)
    sample = x * 2 + zb
    feature = pl.multiple_of(x * 128 + (zb * 2 + z1) * SLICE, SLICE)
    copies = [
        pltpu.make_async_copy(source, target, sems.at[i])
        for i, (source, target) in enumerate(
            [
                (key_weight_ref.at[0, pl.ds(feature, SLICE)], key_weight),
                (value_weight_ref.at[0, pl.ds(feature, SLICE)], value_weight),
                (cot_ref.at[0, sample, heads], cot),
                (out_ref.at[0, sample, heads], out),
                (query_ref.at[0, sample, heads], query),
            ]
        )
    ]
    for copy in copies:
        copy.start()
    longest = length_ref[0]
    for i in range(1, 8):
        longest = jnp.maximum(longest, length_ref[i])
    longest_ref[0] = longest
    copies[0].wait()
    copies[1].wait()
    for g in range(KVH):
        place = 2 * (g % 2 * 4 + g // 2) * HD
        weight_ref[:, place : place + HD] = key_weight[:, g * HD : (g + 1) * HD]
        weight_ref[:, place + HD : place + 2 * HD] = value_weight[:, g * HD : (g + 1) * HD]

    head = lax.broadcasted_iota(jnp.int32, (4, HD), 0)
    place = lax.broadcasted_iota(jnp.int32, (TXT, HD), 0)
    lane = lax.broadcasted_iota(jnp.int32, (TXT, HD), 1)
    twice = jnp.where(lane % TXT == place, 1.0, 0.0).astype(jnp.bfloat16)
    norms = lax.dot_general(norm_ref[0, sample], twice, NN, preferred_element_type=jnp.float32)
    row_mask = jnp.where(place < length_ref[sample], 1.0, 0.0)
    gate = jnp.tanh(jnp.full((TXT, HD), gate_ref[0], jnp.float32))
    row = lax.broadcasted_iota(jnp.int32, (16, HD), 0)
    for copy in copies[2:]:
        copy.wait()
    for i in range(2):
        scaled = (gate * cot[i].astype(jnp.float32) * row_mask).astype(jnp.bfloat16)
        product = scaled.astype(jnp.float32) * out[i].astype(jnp.float32)
        product = jnp.concatenate([product, product], axis=0)
        delta = jnp.sum(product.T, axis=0, keepdims=True)
        norm = jnp.sum(jnp.where(head == 2 * z0 + i, norms, 0.0), axis=0, keepdims=True)
        pack_ref[i, 0:TXT] = query[i]
        pack_ref[i, TXT : 2 * TXT] = scaled
        pack_ref[i, META : META + 16] = jnp.where(
            row == 0, norm, jnp.where(row == 1, delta, 0.0)
        ).astype(jnp.bfloat16)


def prepare(layer_gate, text_lens, query, out, cot, norm, key_weight, value_weight):
    whole = pl.BlockSpec(memory_space=pltpu.HBM)
    vmem = pl.BlockSpec(memory_space=pltpu.VMEM)
    smem = pl.BlockSpec(memory_space=pltpu.SMEM)
    head = pltpu.VMEM((2, TXT, HD), jnp.bfloat16)
    rows = pltpu.VMEM((SLICE, KVH * HD), jnp.bfloat16)
    return pl.pallas_call(
        prepare_kernel,
        in_specs=[smem, smem, whole, whole, whole, vmem, whole, whole],
        out_specs=[vmem, vmem, smem],
        out_shape=[
            jax.ShapeDtypeStruct((2, PACK, HD), jnp.bfloat16),
            jax.ShapeDtypeStruct((SLICE, 2 * KVH * HD), jnp.bfloat16),
            jax.ShapeDtypeStruct((1,), jnp.int32),
        ],
        scratch_shapes=[head, head, head, rows, rows, pltpu.SemaphoreType.DMA((5,))],
        compiler_params=pltpu.CompilerParams(vmem_limit_bytes=WHOLE_VMEM),
        cost_estimate=pl.CostEstimate(flops=1 << 16, bytes_accessed=1 << 18, transcendentals=8192),
    )(layer_gate, text_lens, query, out, cot, norm, key_weight, value_weight)


def split_heads_kernel(key_ref, value_ref, out_ref):
    below = jnp.zeros((PADDED - ROWS, HD), jnp.float32)
    for part, ref in enumerate((key_ref, value_ref)):
        for g in range(KVH):
            head = ref[0, :, g * HD : (g + 1) * HD].astype(jnp.float32)
            head = jnp.concatenate([head, below], axis=0).astype(jnp.bfloat16)
            place = (g // 2 * 2 + part) * HD
            out_ref[g % 2 * 2, :, place : place + HD] = head
            out_ref[g % 2 * 2 + 1, :, place : place + HD] = head


def split_heads(keys, values):
    return pl.pallas_call(
        split_heads_kernel,
        out_shape=jax.ShapeDtypeStruct((4, PADDED, KVH * HD), jnp.bfloat16),
        compiler_params=pltpu.CompilerParams(vmem_limit_bytes=VMEM_LIMIT),
        cost_estimate=pl.CostEstimate(flops=0, bytes_accessed=700000, transcendentals=0),
    )(keys, values)


def attention_kernel(tiles_ref, own_ref, other_ref, heads_ref, out_ref):
    x, zb, z1, z0, zh = (lax.axis_index(name) for name in ("x", "zb", "z1", "z0", "zh"))
    tiles = tiles_ref[x * 2 + zb]
    packs = (own_ref, other_ref)
    query = jnp.concatenate([ref[0, i, 0:TXT] for ref in packs for i in range(2)], axis=0)
    grad = jnp.concatenate([ref[0, i, TXT : 2 * TXT] for ref in packs for i in range(2)], axis=0)
    meta = [ref[0, i, META : META + 16].astype(jnp.float32) for ref in packs for i in range(2)]
    left = lax.broadcasted_iota(jnp.int32, (1, HD), 1) < TXT

    def line(which):
        picked = [meta[i][which : which + 1] for i in range(4)]
        return jnp.concatenate(
            [jnp.where(left, picked[i], picked[i + 1]) for i in range(0, 4, 2)], axis=1
        )

    norm, delta = line(0), line(1)
    line_rows = 4 * PADDED
    wide_row = lax.broadcasted_iota(jnp.int32, (line_rows, GROUP), 0)
    y = sum(jnp.where(wide_row >= i * PADDED, 1, 0) for i in (1, 2, 3))
    row = wide_row - y * PADDED
    position = ((z1 * 2 + z0) * 16 + zh * 4 + y) * ROWS + row
    second = position >= TILE_PAD
    inside = jnp.where(second, position - TILE_PAD, position) < TILE_LEN
    present = jnp.where(second, 1, 0) < tiles
    mask = jnp.where(inside & present & (row < ROWS), 1.0, 0.0)

    def lines(block):
        return block.astype(jnp.float32).reshape(line_rows, HD).astype(jnp.bfloat16)

    keys = lines(heads_ref[:, :, 0:HD])
    values = lines(heads_ref[:, :, HD : 2 * HD])
    scores = lax.dot_general(keys, query, NT, preferred_element_type=jnp.float32) * SCALING
    attention = jnp.exp(scores - norm) * mask
    value_grad = lax.dot_general(
        attention.astype(jnp.bfloat16), grad, NN, preferred_element_type=jnp.float32
    )
    probs = lax.dot_general(values, grad, NT, preferred_element_type=jnp.float32)
    grad_scores = (attention * (probs - delta)).astype(jnp.bfloat16)
    key_grad = lax.dot_general(grad_scores, query, NN, preferred_element_type=jnp.float32) * SCALING
    out_ref[:, :, 0:HD] = key_grad.reshape(4, PADDED, HD).astype(jnp.bfloat16)
    out_ref[:, :, HD : 2 * HD] = value_grad.reshape(4, PADDED, HD).astype(jnp.bfloat16)


def attention_grads(tiles, own, other, heads):
    pack = pl.BlockSpec((1, 2, PACK, HD), lambda s: (s, 0, 0, 0))
    piece = pl.BlockSpec((4, PADDED, 2 * HD), lambda s: (0, 0, s))
    return pl.pallas_call(
        attention_kernel,
        grid=(4,),
        in_specs=[
            pl.BlockSpec(memory_space=pltpu.SMEM),
            pack,
            pack,
            piece,
        ],
        out_specs=piece,
        out_shape=jax.ShapeDtypeStruct((4, PADDED, KVH * HD), jnp.bfloat16),
        compiler_params=pltpu.CompilerParams(vmem_limit_bytes=VMEM_LIMIT),
        cost_estimate=pl.CostEstimate(
            flops=8 * 4 * PADDED * 4 * GROUP * HD,
            bytes_accessed=2 << 20,
            transcendentals=4 * PADDED * 4 * GROUP,
        ),
    )(tiles, own, other, heads)


def project_kernel(grads_ref, weight_ref, out_ref):
    wide = KVH * HD
    total = sum(
        lax.dot_general(
            grads_ref[0, 2 * p : 2 * p + 2].reshape(4 * PADDED, wide),
            weight_ref[:, p * wide : (p + 1) * wide],
            NT,
            preferred_element_type=jnp.float32,
        )
        for p in range(2)
    ).astype(jnp.bfloat16)
    out_ref[0, 0] = total[:, 0:256]
    out_ref[1, 0] = total[:, 256:512]


def project(grads, weight):
    features, depth = weight.shape
    rows = 4 * PADDED
    return pl.pallas_call(
        project_kernel,
        grid=(4,),
        in_specs=[
            pl.BlockSpec((1, 4, rows // 2, depth // 2), lambda x: (x, 0, 0, 0)),
            pl.BlockSpec((features, depth), lambda x: (0, 0)),
        ],
        out_specs=pl.BlockSpec((2, 1, rows, features // 2), lambda x: (0, x, 0, 0)),
        out_shape=jax.ShapeDtypeStruct((2, 4, rows, features // 2), jnp.bfloat16),
        compiler_params=pltpu.CompilerParams(vmem_limit_bytes=WHOLE_VMEM),
        cost_estimate=pl.CostEstimate(
            flops=8 * rows * features * depth, bytes_accessed=7 << 20, transcendentals=0
        ),
    )(grads, weight)


def to_all(array, axes, count):
    copies = jnp.broadcast_to(array[None], (count, *array.shape))
    return lax.all_to_all(copies, axes, split_axis=0, concat_axis=0, tiled=True)


def body(
    text_query,
    attn_out,
    grad_out,
    log_norm,
    image_keys,
    image_values,
    k_weight,
    v_weight,
    layer_gate,
    tile_counts,
    text_lens,
):
    packed, weight, longest = prepare(
        layer_gate, text_lens, text_query, attn_out, grad_out, log_norm, k_weight, v_weight
    )
    weight = lax.all_gather(weight, ("zh", "zb", "z1"), axis=0, tiled=True)
    own = lax.axis_index("y") % 2

    def attend(packed):
        heads = split_heads(image_keys, image_values)
        heads = lax.all_to_all(heads, "y", split_axis=0, concat_axis=0, tiled=True)
        packed = lax.all_gather(packed, "zh", axis=0, tiled=False)
        other = lax.ppermute(packed, "z0", [(0, 1), (1, 0)])
        part = attention_grads(tile_counts, packed, other, heads)
        part = part.reshape(2, 2 * PADDED, KVH * HD)
        kept = lax.dynamic_index_in_dim(part, own, 0, keepdims=False)
        given = lax.dynamic_index_in_dim(part, 1 - own, 0, keepdims=False)
        taken = lax.ppermute(given, "y", [(0, 1), (1, 0), (2, 3), (3, 2)])
        return (kept.astype(jnp.float32) + taken.astype(jnp.float32)).astype(jnp.bfloat16)

    grads = lax.cond(
        longest[0] > 0,
        attend,
        lambda _: jnp.zeros((2 * PADDED, KVH * HD), jnp.bfloat16),
        packed,
    )

    grads = to_all(grads, ("x", "y"), 16).reshape(4, 4, 2 * PADDED, KVH * HD)
    part = project(grads, weight).reshape(32, PADDED, 256)
    part = lax.all_to_all(part, ("core", "x", "y"), split_axis=0, concat_axis=0, tiled=True)
    part = part.reshape(2, 4, 4, PADDED, 2, HD).astype(jnp.float32)
    total = (part[0] + part[1])[:, :, :ROWS]
    return total.transpose(2, 3, 1, 0, 4).reshape(ROWS, 2 * 4 * 4 * HD)


def solution(mesh):
    fine = Mesh(mesh.devices.reshape(SIZES), NAMES)
    tensor = ("zh", "y")
    rows = ("x", "zb", "z1", "z0", "zh", "y")
    in_specs = (
        P("core", None, tensor, None, None),
        P("core", None, tensor, None, None),
        P("core", None, tensor, None, None),
        P("core", None, tensor, None),
        P("core", rows, None),
        P("core", rows, None),
        P("core", tensor, None),
        P("core", tensor, None),
        P("core"),
        P(),
        P(),
    )
    return jax.shard_map(
        body, mesh=fine, in_specs=in_specs, out_specs=P(rows, "core"), check_vma=False
    )
```

```python
import math

import jax
import jax.numpy as jnp
from jax import lax
from jax.experimental import pallas as pl
from jax.experimental.pallas import tpu as pltpu
from jax.sharding import Mesh, PartitionSpec as P

KVH = 8
HD = 128
TXT = 64
TILE_LEN = 1601
TILE_PAD = 1664
NAMES = ("core", "x", "zb", "z1", "z0", "zh", "y")
SIZES = (2, 4, 2, 2, 2, 4, 4)
SCALING = 1.0 / math.sqrt(HD)
META = 2 * TXT
PACK = META + 16
ROWS = 52
PADDED = 56
GROUP = 4 * TXT
SLICE = 32
NT = (((1,), (1,)), ((), ()))
NN = (((1,), (0,)), ((), ()))
VMEM_LIMIT = 16 * 1024 * 1024
WHOLE_VMEM = 60 * 1024 * 1024


def prepare_kernel(
    gate_ref,
    length_ref,
    query_ref,
    out_ref,
    cot_ref,
    norm_ref,
    key_weight_ref,
    value_weight_ref,
    pack_ref,
    weight_ref,
    longest_ref,
    query,
    out,
    cot,
    key_weight,
    value_weight,
    sems,
):
    x, zb, z1, z0 = (lax.axis_index(name) for name in ("x", "zb", "z1", "z0"))
    zq = z1 * 2 + z0
    sample = x * 2 + zb
    feature = pl.multiple_of(x * 128 + (zb * 2 + z1) * SLICE, SLICE)
    copies = [
        pltpu.make_async_copy(source, target, sems.at[i])
        for i, (source, target) in enumerate(
            [
                (key_weight_ref.at[0, pl.ds(feature, SLICE)], key_weight),
                (value_weight_ref.at[0, pl.ds(feature, SLICE)], value_weight),
                (cot_ref.at[0, sample, zq], cot),
                (out_ref.at[0, sample, zq], out),
                (query_ref.at[0, sample, zq], query),
            ]
        )
    ]
    for copy in copies:
        copy.start()
    longest = length_ref[0]
    for i in range(1, 8):
        longest = jnp.maximum(longest, length_ref[i])
    longest_ref[0] = longest
    copies[0].wait()
    copies[1].wait()
    for g in range(KVH):
        place = 2 * (g % 2 * 4 + g // 2) * HD
        weight_ref[:, place : place + HD] = key_weight[:, g * HD : (g + 1) * HD]
        weight_ref[:, place + HD : place + 2 * HD] = value_weight[:, g * HD : (g + 1) * HD]

    head = lax.broadcasted_iota(jnp.int32, (4, HD), 0) == zq
    place = lax.broadcasted_iota(jnp.int32, (TXT, HD), 0)
    lane = lax.broadcasted_iota(jnp.int32, (TXT, HD), 1)
    twice = jnp.where(lane % TXT == place, 1.0, 0.0).astype(jnp.bfloat16)
    norms = lax.dot_general(norm_ref[0, sample], twice, NN, preferred_element_type=jnp.float32)
    norm = jnp.sum(jnp.where(head, norms, 0.0), axis=0, keepdims=True)

    copies[2].wait()
    row_mask = jnp.where(place < length_ref[sample], 1.0, 0.0)
    gate = jnp.tanh(jnp.full((TXT, HD), gate_ref[0], jnp.float32))
    scaled = (gate * cot[...].astype(jnp.float32) * row_mask).astype(jnp.bfloat16)
    pack_ref[TXT : 2 * TXT] = scaled
    copies[3].wait()
    product = scaled.astype(jnp.float32) * out[...].astype(jnp.float32)
    product = jnp.concatenate([product, product], axis=0)
    delta = jnp.sum(product.T, axis=0, keepdims=True)
    row = lax.broadcasted_iota(jnp.int32, (16, HD), 0)
    pack_ref[META : META + 16] = jnp.where(
        row == 0, norm, jnp.where(row == 1, delta, 0.0)
    ).astype(jnp.bfloat16)
    copies[4].wait()
    pack_ref[0:TXT] = query[...]


def prepare(layer_gate, text_lens, query, out, cot, norm, key_weight, value_weight):
    whole = pl.BlockSpec(memory_space=pltpu.HBM)
    vmem = pl.BlockSpec(memory_space=pltpu.VMEM)
    smem = pl.BlockSpec(memory_space=pltpu.SMEM)
    head = pltpu.VMEM((TXT, HD), jnp.bfloat16)
    rows = pltpu.VMEM((SLICE, KVH * HD), jnp.bfloat16)
    return pl.pallas_call(
        prepare_kernel,
        in_specs=[smem, smem, whole, whole, whole, vmem, whole, whole],
        out_specs=[vmem, vmem, smem],
        out_shape=[
            jax.ShapeDtypeStruct((PACK, HD), jnp.bfloat16),
            jax.ShapeDtypeStruct((SLICE, 2 * KVH * HD), jnp.bfloat16),
            jax.ShapeDtypeStruct((1,), jnp.int32),
        ],
        scratch_shapes=[head, head, head, rows, rows, pltpu.SemaphoreType.DMA((5,))],
        compiler_params=pltpu.CompilerParams(vmem_limit_bytes=WHOLE_VMEM),
        cost_estimate=pl.CostEstimate(flops=1 << 16, bytes_accessed=1 << 18, transcendentals=8192),
    )(layer_gate, text_lens, query, out, cot, norm, key_weight, value_weight)


def split_heads_kernel(key_ref, value_ref, out_ref):
    below = jnp.zeros((PADDED - ROWS, HD), jnp.float32)
    for part, ref in enumerate((key_ref, value_ref)):
        for g in range(KVH):
            head = ref[0, :, g * HD : (g + 1) * HD].astype(jnp.float32)
            head = jnp.concatenate([head, below], axis=0).astype(jnp.bfloat16)
            place = (g // 2 * 2 + part) * HD
            out_ref[g % 2 * 2, :, place : place + HD] = head
            out_ref[g % 2 * 2 + 1, :, place : place + HD] = head


def split_heads(keys, values):
    return pl.pallas_call(
        split_heads_kernel,
        out_shape=jax.ShapeDtypeStruct((4, PADDED, KVH * HD), jnp.bfloat16),
        compiler_params=pltpu.CompilerParams(vmem_limit_bytes=VMEM_LIMIT),
        cost_estimate=pl.CostEstimate(flops=0, bytes_accessed=700000, transcendentals=0),
    )(keys, values)


def attention_kernel(tiles_ref, pack_ref, heads_ref, out_ref):
    x, zb, z1, z0, zh = (lax.axis_index(name) for name in ("x", "zb", "z1", "z0", "zh"))
    tiles = tiles_ref[x * 2 + zb]
    query = pack_ref[:, 0, 0:TXT, :].reshape(GROUP, HD)
    grad = pack_ref[:, 0, TXT : 2 * TXT, :].reshape(GROUP, HD)
    meta = pack_ref[:, 0, META : META + 16, :].astype(jnp.float32)
    left = lax.broadcasted_iota(jnp.int32, (1, HD), 1) < TXT

    def line(which):
        picked = [meta[i, which : which + 1] for i in range(4)]
        return jnp.concatenate(
            [jnp.where(left, picked[i], picked[i + 1]) for i in range(0, 4, 2)], axis=1
        )

    norm, delta = line(0), line(1)
    line_rows = 4 * PADDED
    wide_row = lax.broadcasted_iota(jnp.int32, (line_rows, GROUP), 0)
    y = sum(jnp.where(wide_row >= i * PADDED, 1, 0) for i in (1, 2, 3))
    row = wide_row - y * PADDED
    position = ((z1 * 2 + z0) * 16 + zh * 4 + y) * ROWS + row
    second = position >= TILE_PAD
    inside = jnp.where(second, position - TILE_PAD, position) < TILE_LEN
    present = jnp.where(second, 1, 0) < tiles
    mask = jnp.where(inside & present & (row < ROWS), 1.0, 0.0)

    def lines(block):
        return block.astype(jnp.float32).reshape(line_rows, HD).astype(jnp.bfloat16)

    keys = lines(heads_ref[:, :, 0:HD])
    values = lines(heads_ref[:, :, HD : 2 * HD])
    scores = lax.dot_general(keys, query, NT, preferred_element_type=jnp.float32) * SCALING
    attention = jnp.exp(scores - norm) * mask
    value_grad = lax.dot_general(
        attention.astype(jnp.bfloat16), grad, NN, preferred_element_type=jnp.float32
    )
    probs = lax.dot_general(values, grad, NT, preferred_element_type=jnp.float32)
    grad_scores = (attention * (probs - delta)).astype(jnp.bfloat16)
    key_grad = lax.dot_general(grad_scores, query, NN, preferred_element_type=jnp.float32) * SCALING
    out_ref[:, :, 0:HD] = key_grad.reshape(4, PADDED, HD).astype(jnp.bfloat16)
    out_ref[:, :, HD : 2 * HD] = value_grad.reshape(4, PADDED, HD).astype(jnp.bfloat16)


def attention_grads(tiles, packed, heads):
    piece = pl.BlockSpec((4, PADDED, 2 * HD), lambda s: (0, 0, s))
    return pl.pallas_call(
        attention_kernel,
        grid=(4,),
        in_specs=[
            pl.BlockSpec(memory_space=pltpu.SMEM),
            pl.BlockSpec((4, 1, PACK, HD), lambda s: (0, s, 0, 0)),
            piece,
        ],
        out_specs=piece,
        out_shape=jax.ShapeDtypeStruct((4, PADDED, KVH * HD), jnp.bfloat16),
        compiler_params=pltpu.CompilerParams(vmem_limit_bytes=VMEM_LIMIT),
        cost_estimate=pl.CostEstimate(
            flops=8 * 4 * PADDED * 4 * GROUP * HD,
            bytes_accessed=2 << 20,
            transcendentals=4 * PADDED * 4 * GROUP,
        ),
    )(tiles, packed, heads)


def project_kernel(grads_ref, weight_ref, kept_ref, given_ref):
    wide = KVH * HD
    total = sum(
        lax.dot_general(
            grads_ref[0, 2 * p : 2 * p + 2].reshape(4 * PADDED, wide),
            weight_ref[:, p * wide : (p + 1) * wide],
            NT,
            preferred_element_type=jnp.float32,
        )
        for p in range(2)
    )
    first = lax.axis_index("core") == 0
    low, high = total[:, 0:256], total[:, 256:512]
    kept_ref[0] = jnp.where(first, low, high)
    given_ref[0] = jnp.where(first, high, low).astype(jnp.bfloat16)


def project(grads, weight):
    features, depth = weight.shape
    rows = 4 * PADDED
    half = pl.BlockSpec((1, rows, features // 2), lambda x: (x, 0, 0))
    return pl.pallas_call(
        project_kernel,
        grid=(4,),
        in_specs=[
            pl.BlockSpec((1, 4, rows // 2, depth // 2), lambda x: (x, 0, 0, 0)),
            pl.BlockSpec((features, depth), lambda x: (0, 0)),
        ],
        out_specs=[half, half],
        out_shape=[
            jax.ShapeDtypeStruct((4, rows, features // 2), jnp.float32),
            jax.ShapeDtypeStruct((4, rows, features // 2), jnp.bfloat16),
        ],
        compiler_params=pltpu.CompilerParams(vmem_limit_bytes=WHOLE_VMEM),
        cost_estimate=pl.CostEstimate(
            flops=8 * rows * features * depth, bytes_accessed=7 << 20, transcendentals=0
        ),
    )(grads, weight)


def in_columns_kernel(part_ref, out_ref):
    for z in range(2):
        for y in range(4):
            for x in range(4):
                place = (z * 16 + y * 4 + x) * HD
                block = part_ref[x * 4 + y, :, z * HD : (z + 1) * HD].astype(jnp.float32)
                out_ref[:, place : place + HD] = block[0:ROWS]


def in_columns(part):
    return pl.pallas_call(
        in_columns_kernel,
        out_shape=jax.ShapeDtypeStruct((ROWS, 2 * 4 * 4 * HD), jnp.float32),
        compiler_params=pltpu.CompilerParams(vmem_limit_bytes=VMEM_LIMIT),
        cost_estimate=pl.CostEstimate(flops=0, bytes_accessed=1400000, transcendentals=0),
    )(part)


def to_all(array, axes, count):
    copies = jnp.broadcast_to(array[None], (count, *array.shape))
    return lax.all_to_all(copies, axes, split_axis=0, concat_axis=0, tiled=True)


def body(
    text_query,
    attn_out,
    grad_out,
    log_norm,
    image_keys,
    image_values,
    k_weight,
    v_weight,
    layer_gate,
    tile_counts,
    text_lens,
):
    packed, weight, longest = prepare(
        layer_gate, text_lens, text_query, attn_out, grad_out, log_norm, k_weight, v_weight
    )
    weight = lax.all_gather(weight, ("zh", "zb", "z1"), axis=0, tiled=True)
    own = lax.axis_index("y") % 2

    def attend(packed):
        heads = split_heads(image_keys, image_values)
        heads = lax.all_to_all(heads, "y", split_axis=0, concat_axis=0, tiled=True)
        packed = lax.all_gather(packed, "zh", axis=0, tiled=True)
        packed = lax.all_gather(packed, ("z1", "z0"), axis=0, tiled=True)
        packed = packed.reshape(4, 4, PACK, HD)
        part = attention_grads(tile_counts, packed, heads)
        part = part.reshape(2, 2 * PADDED, KVH * HD)
        kept = lax.dynamic_index_in_dim(part, own, 0, keepdims=False)
        given = lax.dynamic_index_in_dim(part, 1 - own, 0, keepdims=False)
        taken = lax.ppermute(given, "y", [(0, 1), (1, 0), (2, 3), (3, 2)])
        return (kept.astype(jnp.float32) + taken.astype(jnp.float32)).astype(jnp.bfloat16)

    grads = lax.cond(
        longest[0] > 0,
        attend,
        lambda _: jnp.zeros((2 * PADDED, KVH * HD), jnp.bfloat16),
        packed,
    )

    grads = to_all(grads, ("x", "y"), 16).reshape(4, 4, 2 * PADDED, KVH * HD)
    kept, given = project(grads, weight)
    taken = lax.ppermute(given, "core", [(0, 1), (1, 0)])
    part = (kept + taken.astype(jnp.float32)).astype(jnp.bfloat16).reshape(16, PADDED, 256)
    part = lax.all_to_all(part, ("x", "y"), split_axis=0, concat_axis=0, tiled=True)
    return in_columns(part)


def solution(mesh):
    fine = Mesh(mesh.devices.reshape(SIZES), NAMES)
    tensor = ("zh", "y")
    rows = ("x", "zb", "z1", "z0", "zh", "y")
    in_specs = (
        P("core", None, tensor, None, None),
        P("core", None, tensor, None, None),
        P("core", None, tensor, None, None),
        P("core", None, tensor, None),
        P("core", rows, None),
        P("core", rows, None),
        P("core", tensor, None),
        P("core", tensor, None),
        P("core"),
        P(),
        P(),
    )
    return jax.shard_map(
        body, mesh=fine, in_specs=in_specs, out_specs=P(rows, "core"), check_vma=False
    )
```

```python
import math

import jax
import jax.numpy as jnp
from jax import lax
from jax.experimental import pallas as pl
from jax.experimental.pallas import tpu as pltpu
from jax.sharding import Mesh, PartitionSpec as P

KVH = 8
HD = 128
TXT = 64
TILE_LEN = 1601
TILE_PAD = 1664
NAMES = ("core", "x", "zb", "z1", "z0", "zh", "y")
SIZES = (2, 4, 2, 2, 2, 4, 4)
SCALING = 1.0 / math.sqrt(HD)
META = 2 * TXT
PACK = META + 16
ROWS = 52
PADDED = 56
GROUP = 4 * TXT
SLICE = 32
NT = (((1,), (1,)), ((), ()))
NN = (((1,), (0,)), ((), ()))
VMEM_LIMIT = 16 * 1024 * 1024
WHOLE_VMEM = 60 * 1024 * 1024


def prepare_kernel(
    gate_ref,
    length_ref,
    query_ref,
    out_ref,
    cot_ref,
    norm_ref,
    key_weight_ref,
    value_weight_ref,
    pack_ref,
    weight_ref,
    longest_ref,
    query,
    out,
    cot,
    key_weight,
    value_weight,
    sems,
):
    x, zb, z1, z0 = (lax.axis_index(name) for name in ("x", "zb", "z1", "z0"))
    zq = z1 * 2 + z0
    sample = x * 2 + zb
    feature = pl.multiple_of(x * 128 + (zb * 2 + z1) * SLICE, SLICE)
    copies = [
        pltpu.make_async_copy(source, target, sems.at[i])
        for i, (source, target) in enumerate(
            [
                (key_weight_ref.at[0, pl.ds(feature, SLICE)], key_weight),
                (value_weight_ref.at[0, pl.ds(feature, SLICE)], value_weight),
                (cot_ref.at[0, sample, zq], cot),
                (out_ref.at[0, sample, zq], out),
                (query_ref.at[0, sample, zq], query),
            ]
        )
    ]
    for copy in copies:
        copy.start()
    longest = length_ref[0]
    for i in range(1, 8):
        longest = jnp.maximum(longest, length_ref[i])
    longest_ref[0] = longest
    copies[0].wait()
    copies[1].wait()
    for g in range(KVH):
        place = 2 * (g % 2 * 4 + g // 2) * HD
        weight_ref[:, place : place + HD] = key_weight[:, g * HD : (g + 1) * HD]
        weight_ref[:, place + HD : place + 2 * HD] = value_weight[:, g * HD : (g + 1) * HD]

    head = lax.broadcasted_iota(jnp.int32, (4, HD), 0) == zq
    place = lax.broadcasted_iota(jnp.int32, (TXT, HD), 0)
    lane = lax.broadcasted_iota(jnp.int32, (TXT, HD), 1)
    twice = jnp.where(lane % TXT == place, 1.0, 0.0).astype(jnp.bfloat16)
    norms = lax.dot_general(norm_ref[0, sample], twice, NN, preferred_element_type=jnp.float32)
    norm = jnp.sum(jnp.where(head, norms, 0.0), axis=0, keepdims=True)

    copies[2].wait()
    row_mask = jnp.where(place < length_ref[sample], 1.0, 0.0)
    gate = jnp.tanh(jnp.full((TXT, HD), gate_ref[0], jnp.float32))
    scaled = (gate * cot[...].astype(jnp.float32) * row_mask).astype(jnp.bfloat16)
    pack_ref[TXT : 2 * TXT] = scaled
    copies[3].wait()
    product = scaled.astype(jnp.float32) * out[...].astype(jnp.float32)
    product = jnp.concatenate([product, product], axis=0)
    delta = jnp.sum(product.T, axis=0, keepdims=True)
    row = lax.broadcasted_iota(jnp.int32, (16, HD), 0)
    pack_ref[META : META + 16] = jnp.where(
        row == 0, norm, jnp.where(row == 1, delta, 0.0)
    ).astype(jnp.bfloat16)
    copies[4].wait()
    pack_ref[0:TXT] = query[...]


def prepare(layer_gate, text_lens, query, out, cot, norm, key_weight, value_weight):
    whole = pl.BlockSpec(memory_space=pltpu.HBM)
    vmem = pl.BlockSpec(memory_space=pltpu.VMEM)
    smem = pl.BlockSpec(memory_space=pltpu.SMEM)
    head = pltpu.VMEM((TXT, HD), jnp.bfloat16)
    rows = pltpu.VMEM((SLICE, KVH * HD), jnp.bfloat16)
    return pl.pallas_call(
        prepare_kernel,
        in_specs=[smem, smem, whole, whole, whole, vmem, whole, whole],
        out_specs=[vmem, vmem, smem],
        out_shape=[
            jax.ShapeDtypeStruct((PACK, HD), jnp.bfloat16),
            jax.ShapeDtypeStruct((SLICE, 2 * KVH * HD), jnp.bfloat16),
            jax.ShapeDtypeStruct((1,), jnp.int32),
        ],
        scratch_shapes=[head, head, head, rows, rows, pltpu.SemaphoreType.DMA((5,))],
        compiler_params=pltpu.CompilerParams(vmem_limit_bytes=WHOLE_VMEM),
        cost_estimate=pl.CostEstimate(flops=1 << 16, bytes_accessed=1 << 18, transcendentals=8192),
    )(layer_gate, text_lens, query, out, cot, norm, key_weight, value_weight)


def split_heads_kernel(key_ref, value_ref, out_ref):
    for part, ref in enumerate((key_ref, value_ref)):
        for g in range(KVH):
            head = ref[0, :, g * HD : (g + 1) * HD]
            place = (g // 2 * 2 + part) * HD
            out_ref[g % 2 * 2, :, place : place + HD] = head
            out_ref[g % 2 * 2 + 1, :, place : place + HD] = head


def split_heads(keys, values):
    return pl.pallas_call(
        split_heads_kernel,
        out_shape=jax.ShapeDtypeStruct((4, ROWS, KVH * HD), jnp.bfloat16),
        compiler_params=pltpu.CompilerParams(vmem_limit_bytes=VMEM_LIMIT),
        cost_estimate=pl.CostEstimate(flops=0, bytes_accessed=700000, transcendentals=0),
    )(keys, values)


def attention_kernel(tiles_ref, pack_ref, heads_ref, out_ref):
    x, zb, z1, z0, zh = (lax.axis_index(name) for name in ("x", "zb", "z1", "z0", "zh"))
    tiles = tiles_ref[x * 2 + zb]
    query = pack_ref[:, 0, 0:TXT, :].reshape(GROUP, HD)
    grad = pack_ref[:, 0, TXT : 2 * TXT, :].reshape(GROUP, HD)
    meta = pack_ref[:, 0, META : META + 16, :].astype(jnp.float32)
    left = lax.broadcasted_iota(jnp.int32, (1, HD), 1) < TXT

    def line(which):
        picked = [meta[i, which : which + 1] for i in range(4)]
        return jnp.concatenate(
            [jnp.where(left, picked[i], picked[i + 1]) for i in range(0, 4, 2)], axis=1
        )

    norm, delta = line(0), line(1)
    line_rows = 4 * ROWS
    wide_row = lax.broadcasted_iota(jnp.int32, (line_rows, GROUP), 0)
    position = ((z1 * 2 + z0) * 16 + zh * 4) * ROWS + wide_row
    second = position >= TILE_PAD
    inside = jnp.where(second, position - TILE_PAD, position) < TILE_LEN
    present = jnp.where(second, 1, 0) < tiles
    mask = jnp.where(inside & present, 1.0, 0.0)

    def lines(block):
        wide = block.astype(jnp.float32)
        return jnp.concatenate([wide[i] for i in range(4)], axis=0).astype(jnp.bfloat16)

    keys = lines(heads_ref[:, :, 0:HD])
    values = lines(heads_ref[:, :, HD : 2 * HD])
    scores = lax.dot_general(keys, query, NT, preferred_element_type=jnp.float32) * SCALING
    attention = jnp.exp(scores - norm) * mask
    value_grad = lax.dot_general(
        attention.astype(jnp.bfloat16), grad, NN, preferred_element_type=jnp.float32
    )
    probs = lax.dot_general(values, grad, NT, preferred_element_type=jnp.float32)
    grad_scores = (attention * (probs - delta)).astype(jnp.bfloat16)
    key_grad = lax.dot_general(grad_scores, query, NN, preferred_element_type=jnp.float32) * SCALING
    out_ref[:, 0:HD] = key_grad.astype(jnp.bfloat16)
    out_ref[:, HD : 2 * HD] = value_grad.astype(jnp.bfloat16)


def attention_grads(tiles, packed, heads):
    piece = pl.BlockSpec((4, ROWS, 2 * HD), lambda s: (0, 0, s))
    return pl.pallas_call(
        attention_kernel,
        grid=(4,),
        in_specs=[
            pl.BlockSpec(memory_space=pltpu.SMEM),
            pl.BlockSpec((4, 1, PACK, HD), lambda s: (0, s, 0, 0)),
            piece,
        ],
        out_specs=pl.BlockSpec((4 * ROWS, 2 * HD), lambda s: (0, s)),
        out_shape=jax.ShapeDtypeStruct((4 * ROWS, KVH * HD), jnp.bfloat16),
        compiler_params=pltpu.CompilerParams(vmem_limit_bytes=VMEM_LIMIT),
        cost_estimate=pl.CostEstimate(
            flops=8 * 4 * ROWS * 4 * GROUP * HD,
            bytes_accessed=2 << 20,
            transcendentals=4 * ROWS * 4 * GROUP,
        ),
    )(tiles, packed, heads)


def project_kernel(grads_ref, weight_ref, kept_ref, given_ref):
    wide = KVH * HD
    total = sum(
        lax.dot_general(
            grads_ref[0, p],
            weight_ref[:, p * wide : (p + 1) * wide],
            NT,
            preferred_element_type=jnp.float32,
        )
        for p in range(2)
    )
    first = lax.axis_index("core") == 0
    low, high = total[:, 0:256], total[:, 256:512]
    kept = jnp.where(first, low, high)
    given = jnp.where(first, high, low)
    below = jnp.zeros((PADDED - ROWS, 256), jnp.float32)
    for y in range(4):
        rows = slice(y * ROWS, (y + 1) * ROWS)
        kept_ref[y] = jnp.concatenate([kept[rows], below], axis=0)
        given_ref[y] = jnp.concatenate([given[rows], below], axis=0).astype(jnp.bfloat16)


def project(grads, weight):
    features, depth = weight.shape
    rows = 4 * ROWS
    half = pl.BlockSpec((4, PADDED, features // 2), lambda x: (x, 0, 0))
    return pl.pallas_call(
        project_kernel,
        grid=(4,),
        in_specs=[
            pl.BlockSpec((1, 2, rows, depth // 2), lambda x: (x, 0, 0, 0)),
            pl.BlockSpec((features, depth), lambda x: (0, 0)),
        ],
        out_specs=[half, half],
        out_shape=[
            jax.ShapeDtypeStruct((16, PADDED, features // 2), jnp.float32),
            jax.ShapeDtypeStruct((16, PADDED, features // 2), jnp.bfloat16),
        ],
        compiler_params=pltpu.CompilerParams(vmem_limit_bytes=WHOLE_VMEM),
        cost_estimate=pl.CostEstimate(
            flops=8 * rows * features * depth, bytes_accessed=7 << 20, transcendentals=0
        ),
    )(grads, weight)


def in_columns_kernel(part_ref, out_ref):
    for z in range(2):
        for y in range(4):
            for x in range(4):
                place = (z * 16 + y * 4 + x) * HD
                block = part_ref[x * 4 + y, :, z * HD : (z + 1) * HD].astype(jnp.float32)
                out_ref[:, place : place + HD] = block[0:ROWS]


def in_columns(part):
    return pl.pallas_call(
        in_columns_kernel,
        out_shape=jax.ShapeDtypeStruct((ROWS, 2 * 4 * 4 * HD), jnp.float32),
        compiler_params=pltpu.CompilerParams(vmem_limit_bytes=VMEM_LIMIT),
        cost_estimate=pl.CostEstimate(flops=0, bytes_accessed=1400000, transcendentals=0),
    )(part)


def to_all(array, axes, count):
    copies = jnp.broadcast_to(array[None], (count, *array.shape))
    return lax.all_to_all(copies, axes, split_axis=0, concat_axis=0, tiled=True)


def body(
    text_query,
    attn_out,
    grad_out,
    log_norm,
    image_keys,
    image_values,
    k_weight,
    v_weight,
    layer_gate,
    tile_counts,
    text_lens,
):
    packed, weight, longest = prepare(
        layer_gate, text_lens, text_query, attn_out, grad_out, log_norm, k_weight, v_weight
    )
    weight = lax.all_gather(weight, ("zh", "zb", "z1"), axis=0, tiled=True)
    own = lax.axis_index("y") % 2

    def attend(packed):
        packed = lax.all_gather(packed, "zh", axis=0, tiled=True)
        packed, keys, values = lax.optimization_barrier((packed, image_keys, image_values))
        heads = split_heads(keys, values)
        heads = lax.all_to_all(heads, "y", split_axis=0, concat_axis=0, tiled=True)
        packed = lax.all_gather(packed, ("z1", "z0"), axis=0, tiled=True)
        packed = packed.reshape(4, 4, PACK, HD)
        part = attention_grads(tile_counts, packed, heads)
        part = part.reshape(2, 2 * ROWS, KVH * HD)
        kept = lax.dynamic_index_in_dim(part, own, 0, keepdims=False)
        given = lax.dynamic_index_in_dim(part, 1 - own, 0, keepdims=False)
        taken = lax.ppermute(given, "y", [(0, 1), (1, 0), (2, 3), (3, 2)])
        return (kept.astype(jnp.float32) + taken.astype(jnp.float32)).astype(jnp.bfloat16)

    grads = lax.cond(
        longest[0] > 0,
        attend,
        lambda _: jnp.zeros((2 * ROWS, KVH * HD), jnp.bfloat16),
        packed,
    )

    grads = to_all(grads, ("x", "y"), 16).reshape(4, 2, 4 * ROWS, KVH * HD)
    kept, given = project(grads, weight)
    taken = lax.ppermute(given, "core", [(0, 1), (1, 0)])
    part = (kept + taken.astype(jnp.float32)).astype(jnp.bfloat16)
    part = lax.all_to_all(part, ("x", "y"), split_axis=0, concat_axis=0, tiled=True)
    return in_columns(part)


def solution(mesh):
    fine = Mesh(mesh.devices.reshape(SIZES), NAMES)
    tensor = ("zh", "y")
    rows = ("x", "zb", "z1", "z0", "zh", "y")
    in_specs = (
        P("core", None, tensor, None, None),
        P("core", None, tensor, None, None),
        P("core", None, tensor, None, None),
        P("core", None, tensor, None),
        P("core", rows, None),
        P("core", rows, None),
        P("core", tensor, None),
        P("core", tensor, None),
        P("core"),
        P(),
        P(),
    )
    return jax.shard_map(
        body, mesh=fine, in_specs=in_specs, out_specs=P(rows, "core"), check_vma=False
    )
```

```python
import math

import jax
import jax.numpy as jnp
from jax import lax
from jax.experimental import pallas as pl
from jax.experimental.pallas import tpu as pltpu
from jax.sharding import Mesh, PartitionSpec as P

KVH = 8
HD = 128
TXT = 64
TILE_LEN = 1601
TILE_PAD = 1664
NAMES = ("core", "x", "zb", "z1", "z0", "zh", "y")
SIZES = (2, 4, 2, 2, 2, 4, 4)
SCALING = 1.0 / math.sqrt(HD)
META = 2 * TXT
PACK = META + 16
ROWS = 52
PADDED = 56
GROUP = 4 * TXT
SLICE = 32
NT = (((1,), (1,)), ((), ()))
NN = (((1,), (0,)), ((), ()))
VMEM_LIMIT = 16 * 1024 * 1024
WHOLE_VMEM = 60 * 1024 * 1024


def prepare_kernel(
    gate_ref,
    length_ref,
    query_ref,
    out_ref,
    cot_ref,
    norm_ref,
    key_weight_ref,
    value_weight_ref,
    pack_ref,
    weight_ref,
    longest_ref,
    query,
    out,
    cot,
    key_weight,
    value_weight,
    sems,
):
    x, zb, z1, z0 = (lax.axis_index(name) for name in ("x", "zb", "z1", "z0"))
    zq = z1 * 2 + z0
    sample = x * 2 + zb
    feature = pl.multiple_of(x * 128 + (zb * 2 + z1) * SLICE, SLICE)
    copies = [
        pltpu.make_async_copy(source, target, sems.at[i])
        for i, (source, target) in enumerate(
            [
                (key_weight_ref.at[0, pl.ds(feature, SLICE)], key_weight),
                (value_weight_ref.at[0, pl.ds(feature, SLICE)], value_weight),
                (cot_ref.at[0, sample, zq], cot),
                (out_ref.at[0, sample, zq], out),
                (query_ref.at[0, sample, zq], query),
            ]
        )
    ]
    for copy in copies:
        copy.start()
    longest = length_ref[0]
    for i in range(1, 8):
        longest = jnp.maximum(longest, length_ref[i])
    longest_ref[0] = longest
    copies[0].wait()
    copies[1].wait()
    for g in range(KVH):
        place = 2 * (g % 2 * 4 + g // 2) * HD
        weight_ref[:, place : place + HD] = key_weight[:, g * HD : (g + 1) * HD]
        weight_ref[:, place + HD : place + 2 * HD] = value_weight[:, g * HD : (g + 1) * HD]

    head = lax.broadcasted_iota(jnp.int32, (4, HD), 0) == zq
    place = lax.broadcasted_iota(jnp.int32, (TXT, HD), 0)
    lane = lax.broadcasted_iota(jnp.int32, (TXT, HD), 1)
    twice = jnp.where(lane % TXT == place, 1.0, 0.0).astype(jnp.bfloat16)
    norms = lax.dot_general(norm_ref[0, sample], twice, NN, preferred_element_type=jnp.float32)
    norm = jnp.sum(jnp.where(head, norms, 0.0), axis=0, keepdims=True)

    copies[2].wait()
    row_mask = jnp.where(place < length_ref[sample], 1.0, 0.0)
    gate = jnp.tanh(jnp.full((TXT, HD), gate_ref[0], jnp.float32))
    scaled = (gate * cot[...].astype(jnp.float32) * row_mask).astype(jnp.bfloat16)
    pack_ref[TXT : 2 * TXT] = scaled
    copies[3].wait()
    product = scaled.astype(jnp.float32) * out[...].astype(jnp.float32)
    product = jnp.concatenate([product, product], axis=0)
    delta = jnp.sum(product.T, axis=0, keepdims=True)
    row = lax.broadcasted_iota(jnp.int32, (16, HD), 0)
    pack_ref[META : META + 16] = jnp.where(
        row == 0, norm, jnp.where(row == 1, delta, 0.0)
    ).astype(jnp.bfloat16)
    copies[4].wait()
    pack_ref[0:TXT] = query[...]


def prepare(layer_gate, text_lens, query, out, cot, norm, key_weight, value_weight):
    whole = pl.BlockSpec(memory_space=pltpu.HBM)
    vmem = pl.BlockSpec(memory_space=pltpu.VMEM)
    smem = pl.BlockSpec(memory_space=pltpu.SMEM)
    head = pltpu.VMEM((TXT, HD), jnp.bfloat16)
    rows = pltpu.VMEM((SLICE, KVH * HD), jnp.bfloat16)
    return pl.pallas_call(
        prepare_kernel,
        in_specs=[smem, smem, whole, whole, whole, vmem, whole, whole],
        out_specs=[vmem, vmem, smem],
        out_shape=[
            jax.ShapeDtypeStruct((PACK, HD), jnp.bfloat16),
            jax.ShapeDtypeStruct((SLICE, 2 * KVH * HD), jnp.bfloat16),
            jax.ShapeDtypeStruct((1,), jnp.int32),
        ],
        scratch_shapes=[head, head, head, rows, rows, pltpu.SemaphoreType.DMA((5,))],
        compiler_params=pltpu.CompilerParams(vmem_limit_bytes=WHOLE_VMEM),
        cost_estimate=pl.CostEstimate(flops=1 << 16, bytes_accessed=1 << 18, transcendentals=8192),
    )(layer_gate, text_lens, query, out, cot, norm, key_weight, value_weight)


def split_heads_kernel(key_ref, value_ref, out_ref):
    for part, ref in enumerate((key_ref, value_ref)):
        for g in range(KVH):
            head = ref[0, :, g * HD : (g + 1) * HD]
            place = (g // 2 * 2 + part) * HD
            out_ref[g % 2 * 2, :, place : place + HD] = head
            out_ref[g % 2 * 2 + 1, :, place : place + HD] = head


def split_heads(keys, values):
    return pl.pallas_call(
        split_heads_kernel,
        out_shape=jax.ShapeDtypeStruct((4, ROWS, KVH * HD), jnp.bfloat16),
        compiler_params=pltpu.CompilerParams(vmem_limit_bytes=VMEM_LIMIT),
        cost_estimate=pl.CostEstimate(flops=0, bytes_accessed=700000, transcendentals=0),
    )(keys, values)


def attention_kernel(tiles_ref, pack_ref, heads_ref, out_ref):
    x, zb, z1, z0, zh = (lax.axis_index(name) for name in ("x", "zb", "z1", "z0", "zh"))
    tiles = tiles_ref[x * 2 + zb]
    query = pack_ref[:, 0, 0:TXT, :].reshape(GROUP, HD)
    grad = pack_ref[:, 0, TXT : 2 * TXT, :].reshape(GROUP, HD)
    meta = pack_ref[:, 0, META : META + 16, :].astype(jnp.float32)
    left = lax.broadcasted_iota(jnp.int32, (1, HD), 1) < TXT

    def line(which):
        picked = [meta[i, which : which + 1] for i in range(4)]
        return jnp.concatenate(
            [jnp.where(left, picked[i], picked[i + 1]) for i in range(0, 4, 2)], axis=1
        )

    norm, delta = line(0), line(1)
    line_rows = 4 * ROWS
    wide_row = lax.broadcasted_iota(jnp.int32, (line_rows, GROUP), 0)
    position = ((z1 * 2 + z0) * 16 + zh * 4) * ROWS + wide_row
    second = position >= TILE_PAD
    inside = jnp.where(second, position - TILE_PAD, position) < TILE_LEN
    present = jnp.where(second, 1, 0) < tiles
    mask = jnp.where(inside & present, 1.0, 0.0)

    def lines(block):
        wide = block.astype(jnp.float32)
        return jnp.concatenate([wide[i] for i in range(4)], axis=0).astype(jnp.bfloat16)

    keys = lines(heads_ref[:, :, 0:HD])
    values = lines(heads_ref[:, :, HD : 2 * HD])
    scores = lax.dot_general(keys, query, NT, preferred_element_type=jnp.float32) * SCALING
    attention = jnp.exp(scores - norm) * mask
    value_grad = lax.dot_general(
        attention.astype(jnp.bfloat16), grad, NN, preferred_element_type=jnp.float32
    )
    probs = lax.dot_general(values, grad, NT, preferred_element_type=jnp.float32)
    grad_scores = (attention * (probs - delta)).astype(jnp.bfloat16)
    key_grad = lax.dot_general(grad_scores, query, NN, preferred_element_type=jnp.float32) * SCALING
    out_ref[:, 0:HD] = key_grad.astype(jnp.bfloat16)
    out_ref[:, HD : 2 * HD] = value_grad.astype(jnp.bfloat16)


def attention_grads(tiles, packed, heads):
    piece = pl.BlockSpec((4, ROWS, 2 * HD), lambda s: (0, 0, s))
    return pl.pallas_call(
        attention_kernel,
        grid=(4,),
        in_specs=[
            pl.BlockSpec(memory_space=pltpu.SMEM),
            pl.BlockSpec((4, 1, PACK, HD), lambda s: (0, s, 0, 0)),
            piece,
        ],
        out_specs=pl.BlockSpec((4 * ROWS, 2 * HD), lambda s: (0, s)),
        out_shape=jax.ShapeDtypeStruct((4 * ROWS, KVH * HD), jnp.bfloat16),
        compiler_params=pltpu.CompilerParams(vmem_limit_bytes=VMEM_LIMIT),
        cost_estimate=pl.CostEstimate(
            flops=8 * 4 * ROWS * 4 * GROUP * HD,
            bytes_accessed=2 << 20,
            transcendentals=4 * ROWS * 4 * GROUP,
        ),
    )(tiles, packed, heads)


def project_kernel(grads_ref, weight_ref, kept_ref, given_ref):
    wide = KVH * HD
    total = sum(
        lax.dot_general(
            jnp.concatenate([grads_ref[x, p] for x in range(2)], axis=0),
            weight_ref[:, p * wide : (p + 1) * wide],
            NT,
            preferred_element_type=jnp.float32,
        )
        for p in range(2)
    )
    first = lax.axis_index("core") == 0
    low, high = total[:, 0:256], total[:, 256:512]
    kept = jnp.where(first, low, high)
    given = jnp.where(first, high, low)
    below = jnp.zeros((PADDED - ROWS, 256), jnp.float32)
    for i in range(8):
        rows = slice(i * ROWS, (i + 1) * ROWS)
        kept_ref[i] = jnp.concatenate([kept[rows], below], axis=0)
        given_ref[i] = jnp.concatenate([given[rows], below], axis=0).astype(jnp.bfloat16)


def project(grads, weight):
    features, depth = weight.shape
    rows = 4 * ROWS
    half = pl.BlockSpec((8, PADDED, features // 2), lambda x: (x, 0, 0))
    return pl.pallas_call(
        project_kernel,
        grid=(2,),
        in_specs=[
            pl.BlockSpec((2, 2, rows, depth // 2), lambda x: (x, 0, 0, 0)),
            pl.BlockSpec((features, depth), lambda x: (0, 0)),
        ],
        out_specs=[half, half],
        out_shape=[
            jax.ShapeDtypeStruct((16, PADDED, features // 2), jnp.float32),
            jax.ShapeDtypeStruct((16, PADDED, features // 2), jnp.bfloat16),
        ],
        compiler_params=pltpu.CompilerParams(vmem_limit_bytes=WHOLE_VMEM),
        cost_estimate=pl.CostEstimate(
            flops=8 * rows * features * depth, bytes_accessed=7 << 20, transcendentals=0
        ),
    )(grads, weight)


def in_columns_kernel(part_ref, out_ref):
    for z in range(2):
        for y in range(4):
            for x in range(4):
                place = (z * 16 + y * 4 + x) * HD
                block = part_ref[x * 4 + y, :, z * HD : (z + 1) * HD].astype(jnp.float32)
                out_ref[:, place : place + HD] = block[0:ROWS]


def in_columns(part):
    return pl.pallas_call(
        in_columns_kernel,
        out_shape=jax.ShapeDtypeStruct((ROWS, 2 * 4 * 4 * HD), jnp.float32),
        compiler_params=pltpu.CompilerParams(vmem_limit_bytes=VMEM_LIMIT),
        cost_estimate=pl.CostEstimate(flops=0, bytes_accessed=1400000, transcendentals=0),
    )(part)


def to_all(array, axes, count):
    copies = jnp.broadcast_to(array[None], (count, *array.shape))
    return lax.all_to_all(copies, axes, split_axis=0, concat_axis=0, tiled=True)


def body(
    text_query,
    attn_out,
    grad_out,
    log_norm,
    image_keys,
    image_values,
    k_weight,
    v_weight,
    layer_gate,
    tile_counts,
    text_lens,
):
    packed, weight, longest = prepare(
        layer_gate, text_lens, text_query, attn_out, grad_out, log_norm, k_weight, v_weight
    )
    weight = lax.all_gather(weight, ("zh", "zb", "z1"), axis=0, tiled=True)
    own = lax.axis_index("y") % 2

    def attend(packed):
        packed = lax.all_gather(packed, "zh", axis=0, tiled=True)
        packed, keys, values = lax.optimization_barrier((packed, image_keys, image_values))
        heads = split_heads(keys, values)
        heads = lax.all_to_all(heads, "y", split_axis=0, concat_axis=0, tiled=True)
        packed = lax.all_gather(packed, ("z1", "z0"), axis=0, tiled=True)
        packed = packed.reshape(4, 4, PACK, HD)
        part = attention_grads(tile_counts, packed, heads)
        part = part.reshape(2, 2 * ROWS, KVH * HD)
        kept = lax.dynamic_index_in_dim(part, own, 0, keepdims=False)
        given = lax.dynamic_index_in_dim(part, 1 - own, 0, keepdims=False)
        taken = lax.ppermute(given, "y", [(0, 1), (1, 0), (2, 3), (3, 2)])
        return (kept.astype(jnp.float32) + taken.astype(jnp.float32)).astype(jnp.bfloat16)

    grads = lax.cond(
        longest[0] > 0,
        attend,
        lambda _: jnp.zeros((2 * ROWS, KVH * HD), jnp.bfloat16),
        packed,
    )

    grads = to_all(grads, ("x", "y"), 16).reshape(4, 2, 4 * ROWS, KVH * HD)
    kept, given = project(grads, weight)
    taken = lax.ppermute(given, "core", [(0, 1), (1, 0)])
    part = (kept + taken.astype(jnp.float32)).astype(jnp.bfloat16)
    part = lax.all_to_all(part, ("x", "y"), split_axis=0, concat_axis=0, tiled=True)
    return in_columns(part)


def solution(mesh):
    fine = Mesh(mesh.devices.reshape(SIZES), NAMES)
    tensor = ("zh", "y")
    rows = ("x", "zb", "z1", "z0", "zh", "y")
    in_specs = (
        P("core", None, tensor, None, None),
        P("core", None, tensor, None, None),
        P("core", None, tensor, None, None),
        P("core", None, tensor, None),
        P("core", rows, None),
        P("core", rows, None),
        P("core", tensor, None),
        P("core", tensor, None),
        P("core"),
        P(),
        P(),
    )
    return jax.shard_map(
        body, mesh=fine, in_specs=in_specs, out_specs=P(rows, "core"), check_vma=False
    )
```

```python
import math

import jax
import jax.numpy as jnp
from jax import lax
from jax.experimental import pallas as pl
from jax.experimental.pallas import tpu as pltpu
from jax.sharding import Mesh, PartitionSpec as P

KVH = 8
HD = 128
TXT = 64
TILE_LEN = 1601
TILE_PAD = 1664
NAMES = ("core", "x", "zb", "z1", "z0", "zh", "y")
SIZES = (2, 4, 2, 2, 2, 4, 4)
SCALING = 1.0 / math.sqrt(HD)
META = 2 * TXT
PACK = META + 16
ROWS = 52
PADDED = 56
GROUP = 4 * TXT
SLICE = 32
NT = (((1,), (1,)), ((), ()))
NN = (((1,), (0,)), ((), ()))
VMEM_LIMIT = 16 * 1024 * 1024
WHOLE_VMEM = 60 * 1024 * 1024


def prepare_kernel(
    gate_ref,
    length_ref,
    query_ref,
    out_ref,
    cot_ref,
    norm_ref,
    key_weight_ref,
    value_weight_ref,
    pack_ref,
    weight_ref,
    longest_ref,
    query,
    out,
    cot,
    key_weight,
    value_weight,
    sems,
):
    x, zb, z1, z0 = (lax.axis_index(name) for name in ("x", "zb", "z1", "z0"))
    zq = z1 * 2 + z0
    sample = x * 2 + zb
    feature = pl.multiple_of(x * 128 + (zb * 2 + z1) * SLICE, SLICE)
    copies = [
        pltpu.make_async_copy(source, target, sems.at[i])
        for i, (source, target) in enumerate(
            [
                (key_weight_ref.at[0, pl.ds(feature, SLICE)], key_weight),
                (value_weight_ref.at[0, pl.ds(feature, SLICE)], value_weight),
                (cot_ref.at[0, sample, zq], cot),
                (out_ref.at[0, sample, zq], out),
                (query_ref.at[0, sample, zq], query),
            ]
        )
    ]
    for copy in copies:
        copy.start()
    longest = length_ref[0]
    for i in range(1, 8):
        longest = jnp.maximum(longest, length_ref[i])
    longest_ref[0] = longest
    copies[0].wait()
    copies[1].wait()
    for g in range(KVH):
        place = 2 * (g % 2 * 4 + g // 2) * HD
        weight_ref[:, place : place + HD] = key_weight[:, g * HD : (g + 1) * HD]
        weight_ref[:, place + HD : place + 2 * HD] = value_weight[:, g * HD : (g + 1) * HD]

    head = lax.broadcasted_iota(jnp.int32, (4, HD), 0) == zq
    place = lax.broadcasted_iota(jnp.int32, (TXT, HD), 0)
    lane = lax.broadcasted_iota(jnp.int32, (TXT, HD), 1)
    twice = jnp.where(lane % TXT == place, 1.0, 0.0).astype(jnp.bfloat16)
    norms = lax.dot_general(norm_ref[0, sample], twice, NN, preferred_element_type=jnp.float32)
    norm = jnp.sum(jnp.where(head, norms, 0.0), axis=0, keepdims=True)

    copies[2].wait()
    row_mask = jnp.where(place < length_ref[sample], 1.0, 0.0)
    gate = jnp.tanh(jnp.full((TXT, HD), gate_ref[0], jnp.float32))
    scaled = (gate * cot[...].astype(jnp.float32) * row_mask).astype(jnp.bfloat16)
    pack_ref[TXT : 2 * TXT] = scaled
    copies[3].wait()
    product = scaled.astype(jnp.float32) * out[...].astype(jnp.float32)
    product = jnp.concatenate([product, product], axis=0)
    delta = jnp.sum(product.T, axis=0, keepdims=True)
    row = lax.broadcasted_iota(jnp.int32, (16, HD), 0)
    pack_ref[META : META + 16] = jnp.where(
        row == 0, norm, jnp.where(row == 1, delta, 0.0)
    ).astype(jnp.bfloat16)
    copies[4].wait()
    pack_ref[0:TXT] = query[...]


def prepare(layer_gate, text_lens, query, out, cot, norm, key_weight, value_weight):
    whole = pl.BlockSpec(memory_space=pltpu.HBM)
    vmem = pl.BlockSpec(memory_space=pltpu.VMEM)
    smem = pl.BlockSpec(memory_space=pltpu.SMEM)
    head = pltpu.VMEM((TXT, HD), jnp.bfloat16)
    rows = pltpu.VMEM((SLICE, KVH * HD), jnp.bfloat16)
    return pl.pallas_call(
        prepare_kernel,
        in_specs=[smem, smem, whole, whole, whole, vmem, whole, whole],
        out_specs=[vmem, vmem, smem],
        out_shape=[
            jax.ShapeDtypeStruct((PACK, HD), jnp.bfloat16),
            jax.ShapeDtypeStruct((SLICE, 2 * KVH * HD), jnp.bfloat16),
            jax.ShapeDtypeStruct((1,), jnp.int32),
        ],
        scratch_shapes=[head, head, head, rows, rows, pltpu.SemaphoreType.DMA((5,))],
        compiler_params=pltpu.CompilerParams(vmem_limit_bytes=WHOLE_VMEM),
        cost_estimate=pl.CostEstimate(flops=1 << 16, bytes_accessed=1 << 18, transcendentals=8192),
    )(layer_gate, text_lens, query, out, cot, norm, key_weight, value_weight)


def split_heads_kernel(key_ref, value_ref, out_ref):
    for part, ref in enumerate((key_ref, value_ref)):
        for g in range(KVH):
            head = ref[0, :, g * HD : (g + 1) * HD]
            place = (g // 2 * 2 + part) * HD
            out_ref[g % 2 * 2, :, place : place + HD] = head
            out_ref[g % 2 * 2 + 1, :, place : place + HD] = head


def split_heads(keys, values):
    return pl.pallas_call(
        split_heads_kernel,
        out_shape=jax.ShapeDtypeStruct((4, ROWS, KVH * HD), jnp.bfloat16),
        compiler_params=pltpu.CompilerParams(vmem_limit_bytes=VMEM_LIMIT),
        cost_estimate=pl.CostEstimate(flops=0, bytes_accessed=700000, transcendentals=0),
    )(keys, values)


def attention_kernel(half_ref, tiles_ref, pack_ref, heads_ref, out_ref):
    x, zb, z1, z0, zh = (lax.axis_index(name) for name in ("x", "zb", "z1", "z0", "zh"))
    tiles = tiles_ref[x * 2 + zb]
    query = pack_ref[:, 0, 0:TXT, :].reshape(GROUP, HD)
    grad = pack_ref[:, 0, TXT : 2 * TXT, :].reshape(GROUP, HD)
    meta = pack_ref[:, 0, META : META + 16, :].astype(jnp.float32)
    left = lax.broadcasted_iota(jnp.int32, (1, HD), 1) < TXT

    def line(which):
        picked = [meta[i, which : which + 1] for i in range(4)]
        return jnp.concatenate(
            [jnp.where(left, picked[i], picked[i + 1]) for i in range(0, 4, 2)], axis=1
        )

    norm, delta = line(0), line(1)
    line_rows = 2 * ROWS
    wide_row = lax.broadcasted_iota(jnp.int32, (line_rows, GROUP), 0)
    position = ((z1 * 2 + z0) * 16 + zh * 4 + 2 * half_ref[0]) * ROWS + wide_row
    second = position >= TILE_PAD
    inside = jnp.where(second, position - TILE_PAD, position) < TILE_LEN
    present = jnp.where(second, 1, 0) < tiles
    mask = jnp.where(inside & present, 1.0, 0.0)

    def lines(block):
        wide = block.astype(jnp.float32)
        return jnp.concatenate([wide[0], wide[1]], axis=0).astype(jnp.bfloat16)

    keys = lines(heads_ref[:, :, 0:HD])
    values = lines(heads_ref[:, :, HD : 2 * HD])
    scores = lax.dot_general(keys, query, NT, preferred_element_type=jnp.float32) * SCALING
    attention = jnp.exp(scores - norm) * mask
    value_grad = lax.dot_general(
        attention.astype(jnp.bfloat16), grad, NN, preferred_element_type=jnp.float32
    )
    probs = lax.dot_general(values, grad, NT, preferred_element_type=jnp.float32)
    grad_scores = (attention * (probs - delta)).astype(jnp.bfloat16)
    key_grad = lax.dot_general(grad_scores, query, NN, preferred_element_type=jnp.float32) * SCALING
    out_ref[:, 0:HD] = key_grad.astype(jnp.bfloat16)
    out_ref[:, HD : 2 * HD] = value_grad.astype(jnp.bfloat16)


def attention_grads(half, tiles, packed, heads):
    return pl.pallas_call(
        attention_kernel,
        grid_spec=pltpu.PrefetchScalarGridSpec(
            num_scalar_prefetch=1,
            grid=(4,),
            in_specs=[
                pl.BlockSpec(memory_space=pltpu.SMEM),
                pl.BlockSpec((4, 1, PACK, HD), lambda s, half: (0, s, 0, 0)),
                pl.BlockSpec((2, ROWS, 2 * HD), lambda s, half: (half[0], 0, s)),
            ],
            out_specs=pl.BlockSpec((2 * ROWS, 2 * HD), lambda s, half: (0, s)),
        ),
        out_shape=jax.ShapeDtypeStruct((2 * ROWS, KVH * HD), jnp.bfloat16),
        compiler_params=pltpu.CompilerParams(vmem_limit_bytes=VMEM_LIMIT),
        cost_estimate=pl.CostEstimate(
            flops=8 * 2 * ROWS * 4 * GROUP * HD,
            bytes_accessed=2 << 20,
            transcendentals=2 * ROWS * 4 * GROUP,
        ),
    )(half.reshape(1), tiles, packed, heads)


def project_kernel(grads_ref, weight_ref, kept_ref, given_ref):
    wide = KVH * HD
    total = sum(
        lax.dot_general(
            jnp.concatenate([grads_ref[x, p] for x in range(2)], axis=0),
            weight_ref[:, p * wide : (p + 1) * wide],
            NT,
            preferred_element_type=jnp.float32,
        )
        for p in range(2)
    )
    first = lax.axis_index("core") == 0
    low, high = total[:, 0:256], total[:, 256:512]
    kept = jnp.where(first, low, high)
    given = jnp.where(first, high, low)
    below = jnp.zeros((PADDED - ROWS, 256), jnp.float32)
    for i in range(8):
        rows = slice(i * ROWS, (i + 1) * ROWS)
        kept_ref[i] = jnp.concatenate([kept[rows], below], axis=0)
        given_ref[i] = jnp.concatenate([given[rows], below], axis=0).astype(jnp.bfloat16)


def project(grads, weight):
    features, depth = weight.shape
    rows = 4 * ROWS
    half = pl.BlockSpec((8, PADDED, features // 2), lambda x: (x, 0, 0))
    return pl.pallas_call(
        project_kernel,
        grid=(2,),
        in_specs=[
            pl.BlockSpec((2, 2, rows, depth // 2), lambda x: (x, 0, 0, 0)),
            pl.BlockSpec((features, depth), lambda x: (0, 0)),
        ],
        out_specs=[half, half],
        out_shape=[
            jax.ShapeDtypeStruct((16, PADDED, features // 2), jnp.float32),
            jax.ShapeDtypeStruct((16, PADDED, features // 2), jnp.bfloat16),
        ],
        compiler_params=pltpu.CompilerParams(vmem_limit_bytes=WHOLE_VMEM),
        cost_estimate=pl.CostEstimate(
            flops=8 * rows * features * depth, bytes_accessed=7 << 20, transcendentals=0
        ),
    )(grads, weight)


def in_columns_kernel(part_ref, out_ref):
    for z in range(2):
        for y in range(4):
            for x in range(4):
                place = (z * 16 + y * 4 + x) * HD
                block = part_ref[x * 4 + y, :, z * HD : (z + 1) * HD].astype(jnp.float32)
                out_ref[:, place : place + HD] = block[0:ROWS]


def in_columns(part):
    return pl.pallas_call(
        in_columns_kernel,
        out_shape=jax.ShapeDtypeStruct((ROWS, 2 * 4 * 4 * HD), jnp.float32),
        compiler_params=pltpu.CompilerParams(vmem_limit_bytes=VMEM_LIMIT),
        cost_estimate=pl.CostEstimate(flops=0, bytes_accessed=1400000, transcendentals=0),
    )(part)


def to_all(array, axes, count):
    copies = jnp.broadcast_to(array[None], (count, *array.shape))
    return lax.all_to_all(copies, axes, split_axis=0, concat_axis=0, tiled=True)


def body(
    text_query,
    attn_out,
    grad_out,
    log_norm,
    image_keys,
    image_values,
    k_weight,
    v_weight,
    layer_gate,
    tile_counts,
    text_lens,
):
    packed, weight, longest = prepare(
        layer_gate, text_lens, text_query, attn_out, grad_out, log_norm, k_weight, v_weight
    )
    weight = lax.all_gather(weight, ("zh", "zb", "z1"), axis=0, tiled=True)
    own = (lax.axis_index("y") % 2).astype(jnp.int32)

    def attend(packed):
        packed = lax.all_gather(packed, "zh", axis=0, tiled=True)
        packed, keys, values = lax.optimization_barrier((packed, image_keys, image_values))
        heads = split_heads(keys, values)
        heads = lax.all_to_all(heads, "y", split_axis=0, concat_axis=0, tiled=True)
        packed = lax.all_gather(packed, ("z1", "z0"), axis=0, tiled=True)
        packed = packed.reshape(4, 4, PACK, HD)
        given = attention_grads(1 - own, tile_counts, packed, heads)
        taken = lax.ppermute(given, "y", [(0, 1), (1, 0), (2, 3), (3, 2)])
        kept = attention_grads(own, tile_counts, packed, heads)
        return (kept.astype(jnp.float32) + taken.astype(jnp.float32)).astype(jnp.bfloat16)

    grads = lax.cond(
        longest[0] > 0,
        attend,
        lambda _: jnp.zeros((2 * ROWS, KVH * HD), jnp.bfloat16),
        packed,
    )

    grads = to_all(grads, ("x", "y"), 16).reshape(4, 2, 4 * ROWS, KVH * HD)
    kept, given = project(grads, weight)
    taken = lax.ppermute(given, "core", [(0, 1), (1, 0)])
    part = (kept + taken.astype(jnp.float32)).astype(jnp.bfloat16)
    part = lax.all_to_all(part, ("x", "y"), split_axis=0, concat_axis=0, tiled=True)
    return in_columns(part)


def solution(mesh):
    fine = Mesh(mesh.devices.reshape(SIZES), NAMES)
    tensor = ("zh", "y")
    rows = ("x", "zb", "z1", "z0", "zh", "y")
    in_specs = (
        P("core", None, tensor, None, None),
        P("core", None, tensor, None, None),
        P("core", None, tensor, None, None),
        P("core", None, tensor, None),
        P("core", rows, None),
        P("core", rows, None),
        P("core", tensor, None),
        P("core", tensor, None),
        P("core"),
        P(),
        P(),
    )
    return jax.shard_map(
        body, mesh=fine, in_specs=in_specs, out_specs=P(rows, "core"), check_vma=False
    )
```

```python
import math

import jax
import jax.numpy as jnp
from jax import lax
from jax.experimental import pallas as pl
from jax.experimental.pallas import tpu as pltpu
from jax.sharding import Mesh, PartitionSpec as P

KVH = 8
HD = 128
TXT = 64
TILE_LEN = 1601
TILE_PAD = 1664
NAMES = ("core", "x", "zb", "z1", "z0", "zh", "y")
SIZES = (2, 4, 2, 2, 2, 4, 4)
SCALING = 1.0 / math.sqrt(HD)
META = 2 * TXT
PACK = META + 16
ROWS = 52
PADDED = 56
GROUP = 4 * TXT
SLICE = 32
NT = (((1,), (1,)), ((), ()))
NN = (((1,), (0,)), ((), ()))
VMEM_LIMIT = 16 * 1024 * 1024
WHOLE_VMEM = 60 * 1024 * 1024


def prepare_kernel(
    gate_ref,
    length_ref,
    query_ref,
    out_ref,
    cot_ref,
    norm_ref,
    key_weight_ref,
    value_weight_ref,
    pack_ref,
    weight_ref,
    longest_ref,
    query,
    out,
    cot,
    key_weight,
    value_weight,
    sems,
):
    x, zb, z1, z0 = (lax.axis_index(name) for name in ("x", "zb", "z1", "z0"))
    zq = z1 * 2 + z0
    sample = x * 2 + zb
    feature = pl.multiple_of(x * 128 + (zb * 2 + z1) * SLICE, SLICE)
    copies = [
        pltpu.make_async_copy(source, target, sems.at[i])
        for i, (source, target) in enumerate(
            [
                (key_weight_ref.at[0, pl.ds(feature, SLICE)], key_weight),
                (value_weight_ref.at[0, pl.ds(feature, SLICE)], value_weight),
                (cot_ref.at[0, sample, zq], cot),
                (out_ref.at[0, sample, zq], out),
                (query_ref.at[0, sample, zq], query),
            ]
        )
    ]
    for copy in copies:
        copy.start()
    longest = length_ref[0]
    for i in range(1, 8):
        longest = jnp.maximum(longest, length_ref[i])
    longest_ref[0] = longest
    copies[0].wait()
    copies[1].wait()
    for g in range(KVH):
        place = 2 * (g % 2 * 4 + g // 2) * HD
        weight_ref[:, place : place + HD] = key_weight[:, g * HD : (g + 1) * HD]
        weight_ref[:, place + HD : place + 2 * HD] = value_weight[:, g * HD : (g + 1) * HD]

    head = lax.broadcasted_iota(jnp.int32, (4, HD), 0) == zq
    place = lax.broadcasted_iota(jnp.int32, (TXT, HD), 0)
    lane = lax.broadcasted_iota(jnp.int32, (TXT, HD), 1)
    twice = jnp.where(lane % TXT == place, 1.0, 0.0).astype(jnp.bfloat16)
    norms = lax.dot_general(norm_ref[0, sample], twice, NN, preferred_element_type=jnp.float32)
    norm = jnp.sum(jnp.where(head, norms, 0.0), axis=0, keepdims=True)

    copies[2].wait()
    row_mask = jnp.where(place < length_ref[sample], 1.0, 0.0)
    gate = jnp.tanh(jnp.full((TXT, HD), gate_ref[0], jnp.float32))
    scaled = (gate * cot[...].astype(jnp.float32) * row_mask).astype(jnp.bfloat16)
    pack_ref[TXT : 2 * TXT] = scaled
    copies[3].wait()
    product = scaled.astype(jnp.float32) * out[...].astype(jnp.float32)
    product = jnp.concatenate([product, product], axis=0)
    delta = jnp.sum(product.T, axis=0, keepdims=True)
    row = lax.broadcasted_iota(jnp.int32, (16, HD), 0)
    pack_ref[META : META + 16] = jnp.where(
        row == 0, norm, jnp.where(row == 1, delta, 0.0)
    ).astype(jnp.bfloat16)
    copies[4].wait()
    pack_ref[0:TXT] = query[...]


def prepare(layer_gate, text_lens, query, out, cot, norm, key_weight, value_weight):
    whole = pl.BlockSpec(memory_space=pltpu.HBM)
    vmem = pl.BlockSpec(memory_space=pltpu.VMEM)
    smem = pl.BlockSpec(memory_space=pltpu.SMEM)
    head = pltpu.VMEM((TXT, HD), jnp.bfloat16)
    rows = pltpu.VMEM((SLICE, KVH * HD), jnp.bfloat16)
    return pl.pallas_call(
        prepare_kernel,
        in_specs=[smem, smem, whole, whole, whole, vmem, whole, whole],
        out_specs=[vmem, vmem, smem],
        out_shape=[
            jax.ShapeDtypeStruct((PACK, HD), jnp.bfloat16),
            jax.ShapeDtypeStruct((SLICE, 2 * KVH * HD), jnp.bfloat16),
            jax.ShapeDtypeStruct((1,), jnp.int32),
        ],
        scratch_shapes=[head, head, head, rows, rows, pltpu.SemaphoreType.DMA((5,))],
        compiler_params=pltpu.CompilerParams(vmem_limit_bytes=WHOLE_VMEM),
        cost_estimate=pl.CostEstimate(flops=1 << 16, bytes_accessed=1 << 18, transcendentals=8192),
    )(layer_gate, text_lens, query, out, cot, norm, key_weight, value_weight)


def split_heads_kernel(key_ref, value_ref, out_ref):
    for part, ref in enumerate((key_ref, value_ref)):
        for g in range(KVH):
            head = ref[0, :, g * HD : (g + 1) * HD]
            place = (g // 2 * 2 + part) * HD
            out_ref[g % 2 * 2, :, place : place + HD] = head
            out_ref[g % 2 * 2 + 1, :, place : place + HD] = head


def split_heads(keys, values):
    return pl.pallas_call(
        split_heads_kernel,
        out_shape=jax.ShapeDtypeStruct((4, ROWS, KVH * HD), jnp.bfloat16),
        compiler_params=pltpu.CompilerParams(vmem_limit_bytes=VMEM_LIMIT),
        cost_estimate=pl.CostEstimate(flops=0, bytes_accessed=700000, transcendentals=0),
    )(keys, values)


def attention_kernel(half_ref, tiles_ref, pack_ref, heads_ref, out_ref):
    x, zb, z1, z0, zh = (lax.axis_index(name) for name in ("x", "zb", "z1", "z0", "zh"))
    tiles = tiles_ref[x * 2 + zb]
    line_rows = 2 * ROWS
    left = lax.broadcasted_iota(jnp.int32, (1, HD), 1) < TXT
    wide_row = lax.broadcasted_iota(jnp.int32, (line_rows, GROUP), 0)
    position = ((z1 * 2 + z0) * 16 + zh * 4 + 2 * half_ref[0]) * ROWS + wide_row
    second = position >= TILE_PAD
    inside = jnp.where(second, position - TILE_PAD, position) < TILE_LEN
    present = jnp.where(second, 1, 0) < tiles
    mask = jnp.where(inside & present, 1.0, 0.0)

    for s in range(2):
        query = pack_ref[:, s, 0:TXT, :].reshape(GROUP, HD)
        grad = pack_ref[:, s, TXT : 2 * TXT, :].reshape(GROUP, HD)
        meta = pack_ref[:, s, META : META + 16, :].astype(jnp.float32)

        def line(which):
            picked = [meta[i, which : which + 1] for i in range(4)]
            return jnp.concatenate(
                [jnp.where(left, picked[i], picked[i + 1]) for i in range(0, 4, 2)], axis=1
            )

        def lines(block):
            wide = block.astype(jnp.float32)
            return jnp.concatenate([wide[0], wide[1]], axis=0).astype(jnp.bfloat16)

        key, value = slice(2 * s * HD, (2 * s + 1) * HD), slice((2 * s + 1) * HD, (2 * s + 2) * HD)
        keys = lines(heads_ref[:, :, key])
        values = lines(heads_ref[:, :, value])
        scores = lax.dot_general(keys, query, NT, preferred_element_type=jnp.float32) * SCALING
        attention = jnp.exp(scores - line(0)) * mask
        value_grad = lax.dot_general(
            attention.astype(jnp.bfloat16), grad, NN, preferred_element_type=jnp.float32
        )
        probs = lax.dot_general(values, grad, NT, preferred_element_type=jnp.float32)
        grad_scores = (attention * (probs - line(1))).astype(jnp.bfloat16)
        key_grad = lax.dot_general(grad_scores, query, NN, preferred_element_type=jnp.float32)
        out_ref[:, key] = (key_grad * SCALING).astype(jnp.bfloat16)
        out_ref[:, value] = value_grad.astype(jnp.bfloat16)


def attention_grads(half, tiles, packed, heads):
    return pl.pallas_call(
        attention_kernel,
        grid_spec=pltpu.PrefetchScalarGridSpec(
            num_scalar_prefetch=1,
            grid=(2,),
            in_specs=[
                pl.BlockSpec(memory_space=pltpu.SMEM),
                pl.BlockSpec((4, 2, PACK, HD), lambda s, half: (0, s, 0, 0)),
                pl.BlockSpec((2, ROWS, 4 * HD), lambda s, half: (half[0], 0, s)),
            ],
            out_specs=pl.BlockSpec((2 * ROWS, 4 * HD), lambda s, half: (0, s)),
        ),
        out_shape=jax.ShapeDtypeStruct((2 * ROWS, KVH * HD), jnp.bfloat16),
        compiler_params=pltpu.CompilerParams(vmem_limit_bytes=VMEM_LIMIT),
        cost_estimate=pl.CostEstimate(
            flops=8 * 2 * ROWS * 4 * GROUP * HD,
            bytes_accessed=2 << 20,
            transcendentals=2 * ROWS * 4 * GROUP,
        ),
    )(half.reshape(1), tiles, packed, heads)


def project_kernel(grads_ref, weight_ref, kept_ref, given_ref):
    wide = KVH * HD
    total = sum(
        lax.dot_general(
            jnp.concatenate([grads_ref[x, p] for x in range(2)], axis=0),
            weight_ref[:, p * wide : (p + 1) * wide],
            NT,
            preferred_element_type=jnp.float32,
        )
        for p in range(2)
    )
    first = lax.axis_index("core") == 0
    low, high = total[:, 0:256], total[:, 256:512]
    kept = jnp.where(first, low, high)
    given = jnp.where(first, high, low)
    below = jnp.zeros((PADDED - ROWS, 256), jnp.float32)
    for i in range(8):
        rows = slice(i * ROWS, (i + 1) * ROWS)
        kept_ref[i] = jnp.concatenate([kept[rows], below], axis=0)
        given_ref[i] = jnp.concatenate([given[rows], below], axis=0).astype(jnp.bfloat16)


def project(grads, weight):
    features, depth = weight.shape
    rows = 4 * ROWS
    half = pl.BlockSpec((8, PADDED, features // 2), lambda x: (x, 0, 0))
    return pl.pallas_call(
        project_kernel,
        grid=(2,),
        in_specs=[
            pl.BlockSpec((2, 2, rows, depth // 2), lambda x: (x, 0, 0, 0)),
            pl.BlockSpec((features, depth), lambda x: (0, 0)),
        ],
        out_specs=[half, half],
        out_shape=[
            jax.ShapeDtypeStruct((16, PADDED, features // 2), jnp.float32),
            jax.ShapeDtypeStruct((16, PADDED, features // 2), jnp.bfloat16),
        ],
        compiler_params=pltpu.CompilerParams(vmem_limit_bytes=WHOLE_VMEM),
        cost_estimate=pl.CostEstimate(
            flops=8 * rows * features * depth, bytes_accessed=7 << 20, transcendentals=0
        ),
    )(grads, weight)


def in_columns_kernel(part_ref, out_ref):
    for z in range(2):
        for y in range(4):
            for x in range(4):
                place = (z * 16 + y * 4 + x) * HD
                block = part_ref[x * 4 + y, :, z * HD : (z + 1) * HD].astype(jnp.float32)
                out_ref[:, place : place + HD] = block[0:ROWS]


def in_columns(part):
    return pl.pallas_call(
        in_columns_kernel,
        out_shape=jax.ShapeDtypeStruct((ROWS, 2 * 4 * 4 * HD), jnp.float32),
        compiler_params=pltpu.CompilerParams(vmem_limit_bytes=VMEM_LIMIT),
        cost_estimate=pl.CostEstimate(flops=0, bytes_accessed=1400000, transcendentals=0),
    )(part)


def to_all(array, axes, count):
    copies = jnp.broadcast_to(array[None], (count, *array.shape))
    return lax.all_to_all(copies, axes, split_axis=0, concat_axis=0, tiled=True)


def body(
    text_query,
    attn_out,
    grad_out,
    log_norm,
    image_keys,
    image_values,
    k_weight,
    v_weight,
    layer_gate,
    tile_counts,
    text_lens,
):
    packed, weight, longest = prepare(
        layer_gate, text_lens, text_query, attn_out, grad_out, log_norm, k_weight, v_weight
    )
    weight = lax.all_gather(weight, ("zh", "zb", "z1"), axis=0, tiled=True)
    own = (lax.axis_index("y") % 2).astype(jnp.int32)

    def attend(packed):
        packed = lax.all_gather(packed, "zh", axis=0, tiled=True)
        packed, keys, values = lax.optimization_barrier((packed, image_keys, image_values))
        heads = split_heads(keys, values)
        heads = lax.all_to_all(heads, "y", split_axis=0, concat_axis=0, tiled=True)
        packed = lax.all_gather(packed, ("z1", "z0"), axis=0, tiled=True)
        packed = packed.reshape(4, 4, PACK, HD)
        given = attention_grads(1 - own, tile_counts, packed, heads)
        taken = lax.ppermute(given, "y", [(0, 1), (1, 0), (2, 3), (3, 2)])
        kept = attention_grads(own, tile_counts, packed, heads)
        return (kept.astype(jnp.float32) + taken.astype(jnp.float32)).astype(jnp.bfloat16)

    grads = lax.cond(
        longest[0] > 0,
        attend,
        lambda _: jnp.zeros((2 * ROWS, KVH * HD), jnp.bfloat16),
        packed,
    )

    grads = to_all(grads, ("x", "y"), 16).reshape(4, 2, 4 * ROWS, KVH * HD)
    kept, given = project(grads, weight)
    taken = lax.ppermute(given, "core", [(0, 1), (1, 0)])
    part = (kept + taken.astype(jnp.float32)).astype(jnp.bfloat16)
    part = lax.all_to_all(part, ("x", "y"), split_axis=0, concat_axis=0, tiled=True)
    return in_columns(part)


def solution(mesh):
    fine = Mesh(mesh.devices.reshape(SIZES), NAMES)
    tensor = ("zh", "y")
    rows = ("x", "zb", "z1", "z0", "zh", "y")
    in_specs = (
        P("core", None, tensor, None, None),
        P("core", None, tensor, None, None),
        P("core", None, tensor, None, None),
        P("core", None, tensor, None),
        P("core", rows, None),
        P("core", rows, None),
        P("core", tensor, None),
        P("core", tensor, None),
        P("core"),
        P(),
        P(),
    )
    return jax.shard_map(
        body, mesh=fine, in_specs=in_specs, out_specs=P(rows, "core"), check_vma=False
    )
```
